32 devices in a mesh: gx: 4 (over y, core), gy: 8 (over z, x).
Axes of the slice: x: 2, y: 2, z: 4, core: 2. Of those that a mesh axis runs over, the one named last changes fastest.
Arguments:
- leaf_values: float32 [4096, 64], P(('gx', 'gy')), may hold values from -6 to 6
- leaf_inverse: bfloat16 [32, 128, 128], P(('gx', 'gy'))
- leaf_coupling: bfloat16 [32, 5, 256, 128], P(('gx', 'gy')), may hold values from -0.5 to 0.5
- block_values: float32 [32, 5, 256, 64], P(('gx', 'gy')), may hold values from -6 to 6
- block_inverse: bfloat16 [32, 5, 256, 256], P(('gx', 'gy'))
- block_coupling: bfloat16 [32, 4, 1, 2, 256, 256], P(('gx', 'gy')), may hold values from -0.375 to 0.375
Outputs:
- leaf_solution: float32 [4096, 64], P(('gx', 'gy'))
- block_solution: float32 [32, 5, 256, 64], P(('gx', 'gy'))
The draws below stay inside these ranges and needn't reach their ends.
All inputs are finite; a program needn't handle non-finite values.
Results may differ from the reference program's by a relative error of at most 0.025.
Values may be sent and summed in bfloat16 or wider, within the bound.
No kernel may reach another device: no remote copies, remote signals or barrier semaphores. Data moves between devices by JAX's collectives and lax.ppermute only.
A program may use at most 64 MiB of HBM per device.

```python
import math
import jax
import jax.numpy as jnp
from jax import lax

W = 256
R = 64
BAND = 1
LEAF = 128
SUBTREES = 32
LEVELS = 5


def draw_leaf_inverse(key, part):
    noise = jax.random.normal(key, (SUBTREES, LEAF, LEAF), jnp.float32)
    return (jnp.eye(LEAF, dtype=jnp.float32) + 0.5 / math.sqrt(LEAF) * noise).astype(jnp.bfloat16)


def draw_block_inverse(key, part):
    noise = jax.random.normal(key, (SUBTREES, LEVELS, W, W), jnp.float32)
    return (jnp.eye(W, dtype=jnp.float32) + 0.5 / math.sqrt(W) * noise).astype(jnp.bfloat16)


def levels(own_key, dims, shards, smallest, largest):
    level, own = 1.0, jax.random.fold_in(own_key, 6)
    for axis_at, blocks in shards:
        steps = jnp.exp(jax.random.uniform(jax.random.fold_in(own, axis_at), (blocks,), jnp.float32, smallest / len(shards), largest / len(shards)))
        level = level * jnp.repeat(steps, dims[axis_at] // blocks).reshape([-1 if axis == axis_at else 1 for axis in range(len(dims))])
    return level


def normal_values(rng, shape, deviation, most, shards=(), kind=jnp.bfloat16):
    values = deviation * jax.random.normal(rng, shape, jnp.float32)
    if shards:
        values = values * levels(rng, shape, shards, -0.22, 0.18)
    return jnp.clip(values, -most, most).astype(kind)


def setup_inputs(seed: int = 0) -> dict:
    splits = jax.random.split(jax.random.key(seed), 7)
    leaf_values = normal_values(splits[0], (SUBTREES * LEAF, R), 1.0, 6.0, ((0, 32),), jnp.float32)
    leaf_inverse = draw_leaf_inverse(jax.random.fold_in(splits[6], 71), 0)
    leaf_coupling = normal_values(splits[2], (SUBTREES, LEVELS, W, LEAF), LEAF ** -0.5, 0.5, ((0, 32),))
    block_values = normal_values(splits[3], (SUBTREES, LEVELS, W, R), 1.0, 6.0, ((0, 32),), jnp.float32)
    block_inverse = draw_block_inverse(jax.random.fold_in(splits[6], 71), 0)
    block_coupling = normal_values(splits[5], (SUBTREES, LEVELS - 1, BAND, 2, W, W), W ** -0.5, 0.375, ((0, 32),))
    return {"leaf_values": leaf_values, "leaf_inverse": leaf_inverse, "leaf_coupling": leaf_coupling, "block_values": block_values, "block_inverse": block_inverse, "block_coupling": block_coupling}


def round_vector(values):
    return lax.optimization_barrier(values.astype(jnp.bfloat16)).astype(jnp.float32)


def apply_block(matrix, values):
    return jnp.einsum("pmn,pnr->pmr", matrix.astype(jnp.float32), round_vector(values), precision=lax.Precision.HIGHEST)


def apply_transpose(matrix, values):
    return jnp.einsum("pnm,pnr->pmr", matrix.astype(jnp.float32), round_vector(values), precision=lax.Precision.HIGHEST)


def reference(leaf_values, leaf_inverse, leaf_coupling, block_values, block_inverse, block_coupling):
    count = SUBTREES
    indices = jnp.arange(count, dtype=jnp.int32)
    leaf_forward = apply_block(leaf_inverse, leaf_values.reshape(count, LEAF, R))
    outgoing = [apply_block(leaf_coupling[:, level], leaf_forward) for level in range(LEVELS)]
    retained = [jnp.zeros((count, W, R), jnp.float32) for level in range(LEVELS)]
    forward = []
    for level in range(LEVELS):
        partner = jnp.bitwise_xor(indices, 1 << level)
        residue = (block_values[:, level] - retained[level]) - outgoing[level][partner]
        solved = apply_block(block_inverse[:, level], residue)
        forward.append(solved)
        for offset in range(BAND):
            upper = level + 1 + offset
            if upper < LEVELS:
                term = jnp.einsum("pswv,pvr->pswr", block_coupling[:, level, offset].astype(jnp.float32), round_vector(solved), precision=lax.Precision.HIGHEST)
                retained[upper] = retained[upper] + term[:, 0]
                outgoing[upper] = outgoing[upper] + term[:, 1]
    backward = [None] * LEVELS
    for level in reversed(range(LEVELS)):
        base = forward[level]
        for offset in range(BAND):
            upper = level + 1 + offset
            if upper < LEVELS:
                other = backward[upper][jnp.bitwise_xor(indices, 1 << upper)]
                stacked = jnp.stack([backward[upper], other], axis=1)
                base = base - jnp.einsum("pswv,pswr->pvr", block_coupling[:, level, offset].astype(jnp.float32), round_vector(stacked), precision=lax.Precision.HIGHEST)
        backward[level] = apply_transpose(block_inverse[:, level], base)
    mirrored = jnp.stack([backward[level][jnp.bitwise_xor(indices, 1 << level)] for level in range(LEVELS)], axis=1)
    gathered = jnp.einsum("pkwn,pkwr->pnr", leaf_coupling.astype(jnp.float32), round_vector(mirrored), precision=lax.Precision.HIGHEST)
    leaf_solution = apply_transpose(leaf_inverse, leaf_forward - gathered)
    return leaf_solution.reshape(count * LEAF, R), jnp.stack(backward, axis=1)
```

```python
import jax
import jax.numpy as jnp
from jax import lax
from jax.experimental import pallas as pl
from jax.experimental.pallas import tpu as pltpu
from jax.sharding import PartitionSpec as P

BF = jnp.bfloat16
F32 = jnp.float32
VMEM = pl.BlockSpec(memory_space=pltpu.VMEM)


def times(values, matrix):
    return lax.dot_general(values, matrix, (((1,), (0,)), ((), ())), preferred_element_type=F32)


def times_t(values, matrix):
    return lax.dot_general(values, matrix, (((1,), (1,)), ((), ())), preferred_element_type=F32)


def gram(left, right):
    return lax.dot_general(left, right, (((0,), (0,)), ((), ())), preferred_element_type=F32)


def from_partner(value, level, gy_levels):
    axis, bit = ("gy", level) if level < gy_levels else ("gx", level - gy_levels)
    mask = 2**bit
    pairs = [(source, source ^ mask) for source in range(lax.axis_size(axis))]
    return lax.ppermute(value, axis, pairs)


def call(body, outs, *args, flops=0):
    moved = sum(a.size * a.dtype.itemsize for a in args)
    return pl.pallas_call(
        body,
        out_shape=[jax.ShapeDtypeStruct(shape, kind) for shape, kind in outs],
        in_specs=[VMEM] * len(args),
        out_specs=[VMEM] * len(outs),
        compiler_params=pltpu.CompilerParams(vmem_limit_bytes=32 * 2**20),
        cost_estimate=pl.CostEstimate(flops=flops, bytes_accessed=moved, transcendentals=0),
    )(*args)


def head(values, inverse, coupling, leaf, out):
    solved = times_t(values[...].astype(BF), inverse[...])
    leaf[...] = solved
    out[...] = times_t(solved.astype(BF), coupling[0]).astype(BF)


def leaf_terms(leaf, coupling, out):
    solved = leaf[...].astype(BF)
    for level in range(1, coupling.shape[0]):
        out[level - 1] = times_t(solved, coupling[level])


def products(inverse, coupling, out, *, level):
    for side in range(2):
        out[side] = times(coupling[level, side], inverse[level]).astype(BF)


def top_gram(inverse, out):
    matrix = inverse[inverse.shape[0] - 1]
    out[...] = gram(matrix, matrix).astype(BF)


def top_products(own, mirror, product, out):
    out[0] = times(own[...], product[0]).astype(BF)
    out[1] = times(mirror[...], product[1]).astype(BF)


def leaf_products(inverse, coupling, out):
    for level in range(coupling.shape[0]):
        out[level] = times(coupling[level], inverse[...]).astype(BF)


def forward(residue, received, product, terms, delta, out, *, level):
    change = (residue[...] - received[...].astype(F32)).astype(BF)
    delta[...] = change
    out[...] = (terms[level] + times_t(change, product[1])).astype(BF)


def forward_side(delta, product, inverse, values, residue, solved, *, level):
    residue[...] = values[level + 1] - times_t(delta[...], product[0])
    step = times_t(delta[...], inverse[level]).astype(BF)
    solved[...] = times(step, inverse[level])


def forward_top(residue, received, product, terms, values, delta, out, *, level):
    change = (residue[...] - received[...].astype(F32)).astype(BF)
    delta[...] = change
    rows = change.shape[0]
    out[:rows] = (terms[level] + times_t(change, product[1])).astype(BF)
    out[rows:] = (values[level + 1] - times_t(change, product[0])).astype(BF)


def solve(delta, inverse, solved, *, level):
    step = times_t(delta[...], inverse[level]).astype(BF)
    solved[...] = times(step, inverse[level])


def top(mine, received, product, solved, out, out_bf, delta):
    rows = solved.shape[0]
    own = (mine[rows:].astype(F32) - received[:rows].astype(F32)).astype(BF)
    other = (received[rows:].astype(F32) - mine[:rows].astype(F32)).astype(BF)
    value = solved[...] - times(own, product[0]) - times(other, product[1])
    out[...] = value
    out_bf[...] = value.astype(BF)
    delta[0] = own
    delta[1] = other


def top_values(delta, own, mirror, out, mirrored):
    out[...] = times(delta[0], own[...])
    mirrored[...] = times(delta[1], mirror[...]).astype(BF)


def back_own(solved, upper, product, out):
    out[...] = solved[...] - times(upper[...], product[0])


def back(own, received, product, out, out_bf):
    value = own[...] - times(received[...], product[1])
    out[...] = value
    out_bf[...] = value.astype(BF)


def leaf_own(leaf, inverse, products_, *refs):
    *mirrored, out = refs
    total = times(leaf[...].astype(BF), inverse[...])
    for level, block in enumerate(mirrored):
        total = total - times(block[...], products_[level + 1])
    out[...] = total


def leaf_last(own, received, products_, out):
    out[...] = own[...] - times(received[...], products_[0])


def gather_blocks(*refs):
    *blocks, out = refs
    for level, block in enumerate(blocks):
        out[level] = block[...]


def shards(leaf_values, leaf_inverse, leaf_coupling, block_values, block_inverse, block_coupling):
    levels, width = block_inverse.shape[1], block_inverse.shape[2]
    size, cols = leaf_values.shape
    gy_levels = lax.axis_size("gy").bit_length() - 1
    inverse, coupling = block_inverse[0], block_coupling[0, :, 0]
    leaf_inv, leaf_cpl = leaf_inverse[0], leaf_coupling[0]
    values = jnp.swapaxes(block_values[0], 1, 2)
    vec, vec_bf, pair = ((cols, width), F32), ((cols, width), BF), ((2, width, width), BF)

    def swap(value, level):
        return from_partner(value, level, gy_levels)

    leaf, out = call(head, [((cols, size), F32), vec_bf], leaf_values.T, leaf_inv, leaf_cpl)
    received = swap(out, 0)
    (terms,) = call(leaf_terms, [((levels - 1, cols, width), F32)], leaf, leaf_cpl)
    product, delta, solved = [], [], []
    residue = values[0]
    own_gram = mirror_gram = None
    for level in range(levels - 1):
        (made,) = call(
            lambda *refs, level=level: products(*refs, level=level), [pair], inverse, coupling
        )
        product.append(made)
        if level == 0:
            (own_gram,) = call(top_gram, [((width, width), BF)], inverse)
        if level < levels - 2:
            change, out = call(
                lambda *refs, level=level: forward(*refs, level=level),
                [vec_bf, vec_bf], residue, received, made, terms,
            )
            received = swap(out, level + 1)
            residue, ahead = call(
                lambda *refs, level=level: forward_side(*refs, level=level),
                [vec, vec], change, made, inverse, values,
            )
            if level == min(1, levels - 3):
                mirror_gram = swap(own_gram, levels - 1)
        else:
            change, out = call(
                lambda *refs, level=level: forward_top(*refs, level=level),
                [vec_bf, ((2 * cols, width), BF)], residue, received, made, terms, values,
            )
            received = swap(out, levels - 1)
            (ahead,) = call(
                lambda *refs, level=level: solve(*refs, level=level), [vec], change, inverse
            )
        delta.append(change)
        solved.append(ahead)
    (top_pair,) = call(top_products, [pair], own_gram, mirror_gram, product[-1])
    (leaf_prod,) = call(leaf_products, [((levels, width, size), BF)], leaf_inv, leaf_cpl)

    blocks, mirrored = [None] * levels, [None] * levels
    block, block_bf, deltas = call(
        top, [vec, vec_bf, ((2, cols, width), BF)], out, received, top_pair, solved[-1]
    )
    blocks[levels - 2] = block
    mirrored[levels - 2] = swap(block_bf, levels - 2)
    blocks[-1], mirrored[-1] = call(top_values, [vec, vec_bf], deltas, own_gram, mirror_gram)
    for level in reversed(range(levels - 2)):
        (own,) = call(back_own, [vec], solved[level], block_bf, product[level])
        block, block_bf = call(back, [vec, vec_bf], own, mirrored[level + 1], product[level])
        blocks[level] = block
        mirrored[level] = swap(block_bf, level)
    (own,) = call(leaf_own, [((cols, size), F32)], leaf, leaf_inv, leaf_prod, *mirrored[1:])
    (stacked,) = call(gather_blocks, [((levels, cols, width), F32)], *blocks)
    (leaf_solution,) = call(leaf_last, [((cols, size), F32)], own, mirrored[0], leaf_prod)
    return leaf_solution.T, jnp.swapaxes(stacked, 1, 2)[None]


def solution(mesh):
    both = ("gx", "gy")
    return jax.shard_map(
        shards,
        mesh=mesh,
        in_specs=tuple(P(both, *[None] * rank) for rank in (1, 2, 3, 3, 3, 5)),
        out_specs=(P(both, None), P(both, None, None, None)),
        check_vma=False,
    )
```

```python
import jax
import jax.numpy as jnp
from jax import lax
from jax.experimental import pallas as pl
from jax.experimental.pallas import tpu as pltpu
from jax.sharding import PartitionSpec as P

BF = jnp.bfloat16
F32 = jnp.float32
VMEM = pl.BlockSpec(memory_space=pltpu.VMEM)


def times(values, matrix):
    return lax.dot_general(values, matrix, (((1,), (0,)), ((), ())), preferred_element_type=F32)


def times_t(values, matrix):
    return lax.dot_general(values, matrix, (((1,), (1,)), ((), ())), preferred_element_type=F32)


def gram(left, right):
    return lax.dot_general(left, right, (((0,), (0,)), ((), ())), preferred_element_type=F32)


def from_partner(value, level, gy_levels):
    axis, bit = ("gy", level) if level < gy_levels else ("gx", level - gy_levels)
    mask = 2**bit
    pairs = [(source, source ^ mask) for source in range(lax.axis_size(axis))]
    return lax.ppermute(value, axis, pairs)


def call(body, outs, *args, flops=3 * 10**8):
    moved = sum(a.size * a.dtype.itemsize for a in args)
    return pl.pallas_call(
        body,
        out_shape=[jax.ShapeDtypeStruct(shape, kind) for shape, kind in outs],
        in_specs=[VMEM] * len(args),
        out_specs=[VMEM] * len(outs),
        compiler_params=pltpu.CompilerParams(vmem_limit_bytes=32 * 2**20),
        cost_estimate=pl.CostEstimate(flops=flops, bytes_accessed=moved, transcendentals=0),
    )(*args)


def products(inverse, coupling, out, *, level):
    for side in range(2):
        out[side] = times(coupling[level, side], inverse[level]).astype(BF)


def top_gram(inverse, out):
    matrix = inverse[inverse.shape[0] - 1]
    out[...] = gram(matrix, matrix).astype(BF)


def top_products(own, mirror, product, out):
    out[0] = times(own[...], product[0]).astype(BF)
    out[1] = times(mirror[...], product[1]).astype(BF)


def forward(residue, received, product, terms, delta, out, *, level):
    change = (residue[0] - received[...].astype(F32)).astype(BF)
    delta[...] = change
    out[...] = (terms[level + 1] + times_t(change, product[1])).astype(BF)


def forward_side(delta, product, inverse, values, residue, solved, *, level):
    residue[0] = values[level + 1] - times_t(delta[...], product[0])
    step = times_t(delta[...], inverse[level]).astype(BF)
    solved[...] = times(step, inverse[level])


def forward_top(residue, received, product, terms, values, delta, out, *, level):
    change = (residue[0] - received[...].astype(F32)).astype(BF)
    delta[...] = change
    rows = change.shape[0]
    out[:rows] = (terms[level + 1] + times_t(change, product[1])).astype(BF)
    out[rows:] = (values[level + 1] - times_t(change, product[0])).astype(BF)


def solve(delta, inverse, solved, *, level):
    step = times_t(delta[...], inverse[level]).astype(BF)
    solved[...] = times(step, inverse[level])


def top(mine, received, product, solved, out, out_bf, delta):
    rows = solved.shape[0]
    own = (mine[rows:].astype(F32) - received[:rows].astype(F32)).astype(BF)
    other = (received[rows:].astype(F32) - mine[:rows].astype(F32)).astype(BF)
    value = solved[...] - times(own, product[0]) - times(other, product[1])
    out[...] = value
    out_bf[...] = value.astype(BF)
    delta[0] = own
    delta[1] = other


def top_values(delta, own, mirror, out, mirrored):
    out[...] = times(delta[0], own[...])
    mirrored[...] = times(delta[1], mirror[...]).astype(BF)


def back_own(solved, upper, product, out):
    out[...] = solved[...] - times(upper[...], product[0])


def back(own, received, product, out, out_bf):
    value = own[...] - times(received[...], product[1])
    out[...] = value
    out_bf[...] = value.astype(BF)


def leaf_own(leaf, inverse, products_, *refs):
    *mirrored, out = refs
    total = times(leaf[...].astype(BF), inverse[...])
    for level, block in enumerate(mirrored):
        total = total - times(block[...], products_[level + 1])
    out[...] = total


def leaf_last(own, received, products_, out):
    out[...] = own[...] - times(received[...], products_[0])


def gather_blocks(*refs):
    *blocks, out = refs
    for level, block in enumerate(blocks):
        out[level] = block[...]


def shards(leaf_values, leaf_inverse, leaf_coupling, block_values, block_inverse, block_coupling):
    levels, width = block_inverse.shape[1], block_inverse.shape[2]
    size, cols = leaf_values.shape
    gy_levels = lax.axis_size("gy").bit_length() - 1
    inverse, coupling = block_inverse[0], block_coupling[0, :, 0]
    leaf_inv, leaf_cpl = leaf_inverse[0], leaf_coupling[0]
    values = jnp.swapaxes(block_values[0], 1, 2)
    vec, vec_bf, pair = ((cols, width), F32), ((cols, width), BF), ((2, width, width), BF)

    def swap(value, level):
        return from_partner(value, level, gy_levels)

    leaf = times_t(leaf_values.T.astype(BF), leaf_inv)
    terms = jnp.einsum("kwn,rn->krw", leaf_cpl, leaf.astype(BF), preferred_element_type=F32)
    received = swap(terms[0].astype(BF), 0)
    product, delta, solved = [], [], []
    residue = values
    own_gram = mirror_gram = None
    for level in range(levels - 1):
        (made,) = call(
            lambda *refs, level=level: products(*refs, level=level), [pair], inverse, coupling
        )
        product.append(made)
        if level == 0:
            (own_gram,) = call(top_gram, [((width, width), BF)], inverse)
        if level < levels - 2:
            change, out = call(
                lambda *refs, level=level: forward(*refs, level=level),
                [vec_bf, vec_bf], residue, received, made, terms,
            )
            received = swap(out, level + 1)
            residue, ahead = call(
                lambda *refs, level=level: forward_side(*refs, level=level),
                [((1, cols, width), F32), vec], change, made, inverse, values,
            )
            if level == min(1, levels - 3):
                own_gram, _ = lax.optimization_barrier((own_gram, out))
                mirror_gram = swap(own_gram, levels - 1)
        else:
            change, out = call(
                lambda *refs, level=level: forward_top(*refs, level=level),
                [vec_bf, ((2 * cols, width), BF)], residue, received, made, terms, values,
            )
            received = swap(out, levels - 1)
            (ahead,) = call(
                lambda *refs, level=level: solve(*refs, level=level), [vec], change, inverse
            )
        delta.append(change)
        solved.append(ahead)
    (top_pair,) = call(top_products, [pair], own_gram, mirror_gram, product[-1])
    leaf_prod = jnp.einsum("kwn,nm->kwm", leaf_cpl, leaf_inv, preferred_element_type=F32).astype(BF)

    blocks, mirrored = [None] * levels, [None] * levels
    block, block_bf, deltas = call(
        top, [vec, vec_bf, ((2, cols, width), BF)], out, received, top_pair, solved[-1]
    )
    blocks[levels - 2] = block
    mirrored[levels - 2] = swap(block_bf, levels - 2)
    blocks[-1], mirrored[-1] = call(top_values, [vec, vec_bf], deltas, own_gram, mirror_gram)
    for level in reversed(range(levels - 2)):
        (own,) = call(back_own, [vec], solved[level], block_bf, product[level])
        block, block_bf = call(back, [vec, vec_bf], own, mirrored[level + 1], product[level])
        blocks[level] = block
        mirrored[level] = swap(block_bf, level)
    (own,) = call(leaf_own, [((cols, size), F32)], leaf, leaf_inv, leaf_prod, *mirrored[1:])
    (stacked,) = call(gather_blocks, [((levels, cols, width), F32)], *blocks)
    (leaf_solution,) = call(leaf_last, [((cols, size), F32)], own, mirrored[0], leaf_prod)
    return leaf_solution.T, jnp.swapaxes(stacked, 1, 2)[None]


def solution(mesh):
    both = ("gx", "gy")
    return jax.shard_map(
        shards,
        mesh=mesh,
        in_specs=tuple(P(both, *[None] * rank) for rank in (1, 2, 3, 3, 3, 5)),
        out_specs=(P(both, None), P(both, None, None, None)),
        check_vma=False,
    )
```

```python
import functools

import jax
import jax.numpy as jnp
from jax import lax
from jax.experimental import pallas as pl
from jax.experimental.pallas import tpu as pltpu
from jax.sharding import PartitionSpec as P

BF = jnp.bfloat16
F32 = jnp.float32
VMEM = pl.BlockSpec(memory_space=pltpu.VMEM)


def times(values, matrix):
    return lax.dot_general(values, matrix, (((1,), (0,)), ((), ())), preferred_element_type=F32)


def times_t(values, matrix):
    return lax.dot_general(values, matrix, (((1,), (1,)), ((), ())), preferred_element_type=F32)


def gram(left, right):
    return lax.dot_general(left, right, (((0,), (0,)), ((), ())), preferred_element_type=F32)


def exchange(value, level, gy_levels, cross=False):
    inner, outer = lax.axis_size("gy"), lax.axis_size("gx")
    mask = 2**level ^ (inner if cross else 0)
    pairs = [(source, source ^ mask) for source in range(inner * outer)]
    return lax.ppermute(value, ("gx", "gy"), pairs)


def call(body, outs, *args, cost=1, **static):
    moved = sum(a.size * a.dtype.itemsize for a in args)
    made = pl.pallas_call(
        functools.partial(body, **static),
        out_shape=[jax.ShapeDtypeStruct(shape, kind) for shape, kind in outs],
        in_specs=[VMEM] * len(args),
        out_specs=[VMEM] * len(outs),
        compiler_params=pltpu.CompilerParams(vmem_limit_bytes=32 * 2**20),
        cost_estimate=pl.CostEstimate(flops=cost * 3 * 10**8, bytes_accessed=moved, transcendentals=0),
    )(*args)
    return made if len(outs) > 1 else made[0]


def products(inverse, coupling, out, *, level):
    for side in range(2):
        out[side] = times(coupling[level, side], inverse[level]).astype(BF)


def products_ahead(inverse, coupling, terms, out, ahead, *, level):
    rows = inverse.shape[1]
    out[0] = times(coupling[level, 0], inverse[level]).astype(BF)
    mirror = times(coupling[level, 1], inverse[level]).astype(BF)
    out[1] = mirror
    ahead[:rows] = mirror
    ahead[rows:] = terms[level + 1].astype(BF)


def top_gram(inverse, out):
    matrix = inverse[inverse.shape[0] - 1]
    out[...] = gram(matrix, matrix).astype(BF)


def top_products(own, mirror, product, out):
    out[0] = times(own[...], product[0]).astype(BF)
    out[1] = times(mirror[...], product[1]).astype(BF)


def forward(residue, received, product, terms, delta, out, *, level):
    change = (residue[0] - received[...].astype(F32)).astype(BF)
    delta[...] = change
    out[...] = (terms[level + 1] + times_t(change, product[1])).astype(BF)


def forward_ahead(residue, received, product, terms, values, delta, out, ahead, *, level):
    change = (residue[0] - received[...].astype(F32)).astype(BF)
    delta[...] = change
    out[...] = (terms[level + 1] + times_t(change, product[1])).astype(BF)
    ahead[...] = (values[level + 1] - times_t(change, product[0])).astype(BF)


def forward_mate(received, residue, ahead, delta, out):
    rows = ahead.shape[1]
    change = (residue[...].astype(F32) - received[...].astype(F32)).astype(BF)
    delta[...] = change
    out[...] = (ahead[rows:].astype(F32) + times_t(change, ahead[:rows])).astype(BF)


def forward_back(received, below, product_below, product, terms, values, delta, out, *, level):
    residue = values[level] - times_t(below[...], product_below[0])
    change = (residue - received[...].astype(F32)).astype(BF)
    delta[...] = change
    out[...] = (terms[level + 1] + times_t(change, product[1])).astype(BF)


def forward_residue(delta, product, values, residue, *, level):
    residue[0] = values[level + 1] - times_t(delta[...], product[0])


def forward_top(residue, received, product, terms, values, delta, out, *, level):
    change = (residue[0] - received[...].astype(F32)).astype(BF)
    delta[...] = change
    rows = change.shape[0]
    out[:rows] = (terms[level + 1] + times_t(change, product[1])).astype(BF)
    out[rows:] = (values[level + 1] - times_t(change, product[0])).astype(BF)


def solve(delta, inverse, solved, *, level):
    step = times_t(delta[...], inverse[level]).astype(BF)
    solved[...] = times(step, inverse[level])


def top(mine, received, product, solved, out, out_bf, delta):
    rows = solved.shape[0]
    own = (mine[rows:].astype(F32) - received[:rows].astype(F32)).astype(BF)
    other = (received[rows:].astype(F32) - mine[:rows].astype(F32)).astype(BF)
    value = solved[...] - times(own, product[0]) - times(other, product[1])
    out[...] = value
    out_bf[...] = value.astype(BF)
    delta[0] = own
    delta[1] = other


def top_values(delta, own, mirror, out, mirrored):
    out[...] = times(delta[0], own[...])
    mirrored[...] = times(delta[1], mirror[...]).astype(BF)


def back_part(solved, known, product, out, *, side):
    out[...] = solved[...] - times(known[...].astype(BF), product[side])


def back(part, received, product, *outs, side):
    value = part[...] - times(received[...].astype(BF), product[side])
    for out in outs:
        out[...] = value.astype(out.dtype)


def back_both(received, known, solved, product, *outs):
    value = solved[...] - times(known[...], product[0])
    value = value - times(received[...].astype(BF), product[1])
    for out in outs:
        out[...] = value.astype(out.dtype)


def leaf_part(leaf, inverse, leaf_products, *refs, early):
    *mirrored, out = refs
    total = times(leaf[...].astype(BF), inverse[...])
    for level, block in zip(early, mirrored, strict=True):
        total = total - times(block[...], leaf_products[level])
    out[...] = total


def finish(part, leaf_products, *refs, late):
    *refs, leaf, out = refs
    mirrored, blocks = refs[: len(late)], refs[len(late) :]
    total = part[...]
    for level, block in zip(late, mirrored, strict=True):
        total = total - times(block[...].astype(BF), leaf_products[level])
    leaf[...] = total
    for level, block in enumerate(blocks):
        out[level] = block[...].astype(F32)


def shards(leaf_values, leaf_inverse, leaf_coupling, block_values, block_inverse, block_coupling):
    levels, width = block_inverse.shape[1], block_inverse.shape[2]
    size, cols = leaf_values.shape
    core = lax.axis_size("gy").bit_length() - 1
    inverse, coupling = block_inverse[0], block_coupling[0, :, 0]
    leaf_inv, leaf_cpl = leaf_inverse[0], leaf_coupling[0]
    values = jnp.swapaxes(block_values[0], 1, 2)
    vec, vec_bf, pair = ((cols, width), F32), ((cols, width), BF), ((2, width, width), BF)
    slab = ((1, cols, width), F32)

    def send(value, level, cross=False):
        return exchange(value, level, core, cross)

    def mate(value):
        return exchange(value, core, core)

    def arrived(value):
        return value.astype(F32)

    def after(value, other):
        return lax.optimization_barrier((value, other))[0]

    below_top = levels - 1
    first_across = 1 + (core - 1) % 2
    at_home = [
        level < first_across or level >= core or (level - first_across) % 2 == 1
        for level in range(levels)
    ]
    leaf = times_t(leaf_values.T.astype(BF), leaf_inv)
    terms = jnp.einsum("kwn,rn->krw", leaf_cpl, leaf.astype(BF), preferred_element_type=F32)
    received = send(terms[0].astype(BF), 0)
    product, ahead, solved = [None] * below_top, [None] * below_top, [None] * below_top
    own_gram = call(top_gram, [((width, width), BF)], inverse)
    inverse = after(inverse, own_gram)
    for level in range(below_top):
        if at_home[level]:
            product[level] = call(products, [pair], inverse, coupling, level=level, cost=1 if level < 2 else 1)
        else:
            product[level], ahead[level] = call(
                products_ahead, [pair, ((width + cols, width), BF)], inverse, coupling, terms, level=level
            )

    residue, change = values, None
    for level in range(below_top):
        below = change
        if level == levels - 2:
            received, mirror_gram = lax.optimization_barrier((received, mirror_gram))
            change, out = call(
                forward_top, [vec_bf, ((2 * cols, width), BF)],
                residue, received, product[level], terms, values, level=level,
            )
            received = send(out, below_top)
        else:
            across = first_across <= level + 1 < core
            if not at_home[level]:
                change, out = call(forward_mate, [vec_bf, vec_bf], arrived(received), residue, ahead[level])
            elif level and not at_home[level - 1]:
                change, out = call(
                    forward_back, [vec_bf, vec_bf], arrived(received), below,
                    product[level - 1], product[level], terms, values, level=level, cost=1,
                )
            elif not at_home[level + 1]:
                change, out, residue = call(
                    forward_ahead, [vec_bf, vec_bf, vec_bf],
                    residue, received, product[level], terms, values, level=level,
                )
            else:
                change, out = call(
                    forward, [vec_bf, vec_bf], residue, received, product[level], terms, level=level
                )
            received = send(out, level + 1, across)
            if level == 0:
                mirror_gram = send(after(own_gram, out), below_top)
            if not at_home[level]:
                change = mate(change)
            elif not at_home[level + 1]:
                residue = mate(residue)
                ahead[level + 1] = mate(after(ahead[level + 1], out))
            else:
                residue = call(
                    forward_residue, [slab], change, product[level], values, level=level, cost=0
                )
        solved[level] = call(solve, [vec], change, inverse, level=level)
    top_pair = call(top_products, [pair], own_gram, mirror_gram, product[-1], cost=8)
    leaf_prod = jnp.einsum("kwn,nm->kwm", leaf_cpl, leaf_inv, preferred_element_type=F32).astype(BF)

    mates = [level for level in range(core) if level % 2 == 0]
    for level in mates:
        product[level] = mate(after(product[level], out))
        solved[level] = mate(after(solved[level], out))
    blocks, mirrored = [None] * levels, [None] * levels
    block, block_bf, deltas = call(
        top, [vec, vec_bf, ((2, cols, width), BF)], out, received, top_pair, solved[-1]
    )
    blocks[levels - 2] = block
    received = mirrored[levels - 2] = send(block_bf, levels - 2)
    blocks[-1], mirrored[-1] = call(top_values, [vec, vec_bf], deltas, own_gram, mirror_gram)
    late = [0]
    for level in reversed(range(levels - 2)):
        home = level not in mates
        outs = [vec, vec_bf] if home else [vec_bf]
        if level + 1 >= core:
            side = 0 if home else 1
            part = call(back_part, [vec], solved[level], block_bf, product[level], side=side)
            made = call(back, outs, part, received, product[level], side=1 - side)
        else:
            known = mate(block_bf)
            if home:
                blocks[level + 1] = known
            made = call(back_both, outs, arrived(received), known, solved[level], product[level])
        if home:
            blocks[level], block_bf = made
        else:
            block_bf = made
        received = send(block_bf, level, level < core)
        if home == (level < core):
            mirrored[level] = mate(received)
            late.append(level)
        else:
            mirrored[level] = received
    if 0 in mates:
        blocks[0] = mate(block_bf)
    early = tuple(level for level in range(levels) if level not in late)
    part = call(
        leaf_part, [((cols, size), F32)],
        leaf, leaf_inv, leaf_prod, *[mirrored[level] for level in early], early=early,
    )
    mirrored[0] = arrived(mirrored[0])
    leaf_solution, stacked = call(
        finish, [((cols, size), F32), ((levels, cols, width), F32)],
        part, leaf_prod, *[mirrored[level] for level in late], *blocks, late=tuple(late),
    )
    return leaf_solution.T, jnp.swapaxes(stacked, 1, 2)[None]


def solution(mesh):
    both = ("gx", "gy")
    return jax.shard_map(
        shards,
        mesh=mesh,
        in_specs=tuple(P(both, *[None] * rank) for rank in (1, 2, 3, 3, 3, 5)),
        out_specs=(P(both, None), P(both, None, None, None)),
        check_vma=False,
    )
```

```python
import functools

import jax
import jax.numpy as jnp
from jax import lax
from jax.experimental import pallas as pl
from jax.experimental.pallas import tpu as pltpu
from jax.sharding import PartitionSpec as P

BF = jnp.bfloat16
F32 = jnp.float32
VMEM = pl.BlockSpec(memory_space=pltpu.VMEM)


def times(values, matrix):
    return lax.dot_general(values, matrix, (((1,), (0,)), ((), ())), preferred_element_type=F32)


def times_t(values, matrix):
    return lax.dot_general(values, matrix, (((1,), (1,)), ((), ())), preferred_element_type=F32)


def gram(left, right):
    return lax.dot_general(left, right, (((0,), (0,)), ((), ())), preferred_element_type=F32)


def exchange(value, level, gy_levels, cross=False):
    inner, outer = lax.axis_size("gy"), lax.axis_size("gx")
    mask = 2**level ^ (inner if cross else 0)
    pairs = [(source, source ^ mask) for source in range(inner * outer)]
    return lax.ppermute(value, ("gx", "gy"), pairs)


def call(body, outs, *args, cost=1, **static):
    moved = sum(a.size * a.dtype.itemsize for a in args)
    made = pl.pallas_call(
        functools.partial(body, **static),
        out_shape=[jax.ShapeDtypeStruct(shape, kind) for shape, kind in outs],
        in_specs=[VMEM] * len(args),
        out_specs=[VMEM] * len(outs),
        compiler_params=pltpu.CompilerParams(vmem_limit_bytes=32 * 2**20),
        cost_estimate=pl.CostEstimate(flops=cost * 3 * 10**8, bytes_accessed=moved, transcendentals=0),
    )(*args)
    return made if len(outs) > 1 else made[0]


def products(inverse, coupling, out, *, level):
    for side in range(2):
        out[side] = times(coupling[level, side], inverse[level]).astype(BF)


def products_ahead(inverse, coupling, terms, out, ahead, *, level):
    rows = inverse.shape[1]
    out[0] = times(coupling[level, 0], inverse[level]).astype(BF)
    mirror = times(coupling[level, 1], inverse[level]).astype(BF)
    out[1] = mirror
    ahead[:rows] = mirror
    ahead[rows:] = terms[level + 1].astype(BF)


def top_gram(inverse, out):
    matrix = inverse[inverse.shape[0] - 1]
    out[...] = gram(matrix, matrix).astype(BF)


def top_products(own, mirror, product, out):
    out[0] = times(own[...], product[0]).astype(BF)
    out[1] = times(mirror[...], product[1]).astype(BF)


def forward(residue, received, product, terms, delta, out, *, level):
    change = (residue[0] - received[...].astype(F32)).astype(BF)
    delta[...] = change
    out[...] = (terms[level + 1] + times_t(change, product[1])).astype(BF)


def forward_ahead(residue, received, product, terms, values, delta, out, ahead, *, level):
    change = (residue[0] - received[...].astype(F32)).astype(BF)
    delta[...] = change
    out[...] = (terms[level + 1] + times_t(change, product[1])).astype(BF)
    ahead[...] = (values[level + 1] - times_t(change, product[0])).astype(BF)


def forward_mate(received, residue, ahead, delta, out):
    rows = ahead.shape[1]
    change = (residue[...].astype(F32) - received[...].astype(F32)).astype(BF)
    delta[...] = change
    out[...] = (ahead[rows:].astype(F32) + times_t(change, ahead[:rows])).astype(BF)


def forward_back(received, below, product_below, product, terms, values, delta, out, *, level):
    residue = values[level] - times_t(below[...], product_below[0])
    change = (residue - received[...].astype(F32)).astype(BF)
    delta[...] = change
    out[...] = (terms[level + 1] + times_t(change, product[1])).astype(BF)


def forward_residue(delta, product, values, residue, *, level):
    residue[0] = values[level + 1] - times_t(delta[...], product[0])


def forward_top(residue, received, product, terms, values, delta, out, *, level):
    change = (residue[0] - received[...].astype(F32)).astype(BF)
    delta[...] = change
    rows = change.shape[0]
    out[:rows] = (terms[level + 1] + times_t(change, product[1])).astype(BF)
    out[rows:] = (values[level + 1] - times_t(change, product[0])).astype(BF)


def forward_first(residue, received, inverse, coupling, terms, values, delta, out, ahead):
    change = (residue[0] - received[...].astype(F32)).astype(BF)
    delta[...] = change
    step = times_t(change, inverse[0]).astype(BF)
    out[...] = (terms[1] + times_t(step, coupling[0, 1])).astype(BF)
    ahead[...] = (values[1] - times_t(step, coupling[0, 0])).astype(BF)


def forward_last(received, below, product_below, product, terms, values, delta, out, *, level):
    residue = values[level] - times_t(below[...], product_below[0])
    change = (residue - received[...].astype(F32)).astype(BF)
    delta[...] = change
    rows = change.shape[0]
    out[:rows] = (terms[level + 1] + times_t(change, product[1])).astype(BF)
    out[rows:] = (values[level + 1] - times_t(change, product[0])).astype(BF)


def pack_top(own_gram, inverse, coupling, out, *, level):
    width = inverse.shape[1]
    out[:width] = own_gram[...]
    for side in range(2):
        made = times(coupling[level, side], inverse[level]).astype(BF)
        out[(side + 1) * width : (side + 2) * width] = made


def top_ends(terms, values, out):
    cols = values.shape[1]
    out[:cols] = values[values.shape[0] - 1].astype(BF)
    out[cols:] = terms[terms.shape[0] - 1].astype(BF)


def join_top(mine, mirror, ends, mirror_ends, inverse, out, *, level):
    width = inverse.shape[1]
    gram_mine, gram_mirror = mine[:width], mirror[:width]
    own, other = mine[width : 2 * width], mine[2 * width : 3 * width]
    mirror_own, mirror_other = mirror[width : 2 * width], mirror[2 * width : 3 * width]
    first = times(gram_mine, own).astype(BF)
    second = times(gram_mirror, other).astype(BF)
    matrix = inverse[level]
    out[:width] = (gram(matrix, matrix) + gram(own, first) + gram(other, second)).astype(BF)
    out[width : 2 * width] = (gram(mirror_other, first) + gram(mirror_own, second)).astype(BF)
    right, mirror_right = top_rights(ends, mirror_ends)
    out[2 * width :] = (-times(right, first) - times(mirror_right, second)).astype(BF)


def top_rights(mine, mirror):
    cols = mine.shape[0] // 2
    right = mine[:cols].astype(F32) - mirror[cols:].astype(F32)
    mirror_right = mirror[:cols].astype(F32) - mine[cols:].astype(F32)
    return right.astype(BF), mirror_right.astype(BF)


def join_own(mine, mate, joined, joined_mate, out, delta):
    rows, width = out.shape[1], joined.shape[1]
    for at, (a, b, matrices) in enumerate(((mine, mate, joined), (mate, mine, joined_mate))):
        change = (a[rows:].astype(F32) - b[:rows].astype(F32)).astype(BF)
        delta[at] = change
        out[at] = times(change, matrices[:width]) + matrices[2 * width :].astype(F32)


def join(theirs, across, part, joined, joined_mate, solved, product, block, block_mate, delta, below, *, home):
    rows, width = part.shape[1], joined.shape[1]
    found = []
    pairs = ((theirs, across, joined), (across, theirs, joined_mate))
    for at, (a, b, matrices) in enumerate(pairs):
        change = (a[rows:].astype(F32) - b[:rows].astype(F32)).astype(BF)
        value = part[at] + times(change, matrices[width : 2 * width])
        found.append(value.astype(BF))
        if at == 0:
            block[...] = value
            delta[0] = change
    block_mate[...] = found[1]
    own, other = found if home else found[::-1]
    below[...] = (solved[...] - times(own, product[0]) - times(other, product[1])).astype(BF)


def top_blocks(mine, mirror, ends, mirror_ends, delta, delta_mirror, out, mirrored):
    width = out.shape[1]
    right, mirror_right = top_rights(ends, mirror_ends)
    change, other = delta[0], delta_mirror[0]
    own = right.astype(F32) - times_t(change, mine[width : 2 * width])
    own = own - times_t(other, mirror[2 * width : 3 * width])
    theirs = mirror_right.astype(F32) - times_t(other, mirror[width : 2 * width])
    theirs = theirs - times_t(change, mine[2 * width : 3 * width])
    out[...] = times(own.astype(BF), mine[:width])
    mirrored[...] = times(theirs.astype(BF), mirror[:width]).astype(BF)


def solve(delta, inverse, solved, *, level):
    step = times_t(delta[...], inverse[level]).astype(BF)
    solved[...] = times(step, inverse[level])


def top(mine, received, product, solved, out, out_bf, delta):
    rows = solved.shape[0]
    own = (mine[rows:].astype(F32) - received[:rows].astype(F32)).astype(BF)
    other = (received[rows:].astype(F32) - mine[:rows].astype(F32)).astype(BF)
    value = solved[...] - times(own, product[0]) - times(other, product[1])
    out[...] = value
    out_bf[...] = value.astype(BF)
    delta[0] = own
    delta[1] = other


def top_values(delta, own, mirror, out, mirrored):
    out[...] = times(delta[0], own[...])
    mirrored[...] = times(delta[1], mirror[...]).astype(BF)


def back_part(solved, known, product, out, *, side):
    out[...] = solved[...] - times(known[...].astype(BF), product[side])


def back(part, received, product, *outs, side):
    value = part[...] - times(received[...].astype(BF), product[side])
    for out in outs:
        out[...] = value.astype(out.dtype)


def back_both(received, known, solved, product, *outs):
    value = solved[...] - times(known[...], product[0])
    value = value - times(received[...].astype(BF), product[1])
    for out in outs:
        out[...] = value.astype(out.dtype)


def leaf_part(leaf, inverse, leaf_products, *refs, early):
    *mirrored, out = refs
    total = times(leaf[...].astype(BF), inverse[...])
    for level, block in zip(early, mirrored, strict=True):
        total = total - times(block[...], leaf_products[level])
    out[...] = total


def finish(part, leaf_products, *refs, late):
    *refs, leaf, out = refs
    mirrored, blocks = refs[: len(late)], refs[len(late) :]
    total = part[...]
    for level, block in zip(late, mirrored, strict=True):
        total = total - times(block[...].astype(BF), leaf_products[level])
    leaf[...] = total
    for level, block in enumerate(blocks):
        out[level] = block[...].astype(F32)


def shards(leaf_values, leaf_inverse, leaf_coupling, block_values, block_inverse, block_coupling):
    levels, width = block_inverse.shape[1], block_inverse.shape[2]
    size, cols = leaf_values.shape
    core = lax.axis_size("gy").bit_length() - 1
    inverse, coupling = block_inverse[0], block_coupling[0, :, 0]
    leaf_inv, leaf_cpl = leaf_inverse[0], leaf_coupling[0]
    values = jnp.swapaxes(block_values[0], 1, 2)
    vec, vec_bf, pair = ((cols, width), F32), ((cols, width), BF), ((2, width, width), BF)
    slab = ((1, cols, width), F32)

    def send(value, level, cross=False):
        return exchange(value, level, core, cross)

    def mate(value):
        return exchange(value, core, core)

    def arrived(value):
        return value.astype(F32)

    def after(value, other):
        return lax.optimization_barrier((value, other))[0]

    below_top = levels - 1
    first_across = 1 + (core - 1) % 2
    at_home = [
        level < first_across or level >= core or (level - first_across) % 2 == 1
        for level in range(levels)
    ]
    leaf = times_t(leaf_values.T.astype(BF), leaf_inv)
    terms = jnp.einsum("kwn,rn->krw", leaf_cpl, leaf.astype(BF), preferred_element_type=F32)
    received = send(terms[0].astype(BF), 0)
    product, ahead, solved = [None] * below_top, [None] * below_top, [None] * below_top
    joined = levels == core + 2 and core >= 3
    own_gram = call(top_gram, [((width, width), BF)], inverse)
    inverse_later = after(inverse, own_gram)
    if joined:
        pack = call(
            pack_top, [((3 * width, width), BF)], own_gram, inverse_later, coupling, level=core
        )
        mirror_pack = send(pack, below_top)
        inverse_later = after(inverse, pack)
        ends = call(top_ends, [((2 * cols, width), BF)], terms, values)
    for level in range(core if joined else below_top):
        if at_home[level]:
            product[level] = call(products, [pair], inverse_later, coupling, level=level, cost=(6, 1, 1)[min(level, 2)])
        else:
            product[level], ahead[level] = call(
                products_ahead, [pair, ((width + cols, width), BF)],
                inverse_later, coupling, terms, level=level,
            )

    residue, change = values, None
    for level in range(core if joined else below_top):
        below = change
        if joined and level == core - 1:
            change, out = call(
                forward_last, [vec_bf, ((2 * cols, width), BF)], arrived(received), below,
                product[level - 1], product[level], terms, values, level=level, cost=4,
            )
            received = send(out, below_top, True)
        elif level == levels - 2:
            received, mirror_gram = lax.optimization_barrier((received, mirror_gram))
            change, out = call(
                forward_top, [vec_bf, ((2 * cols, width), BF)],
                residue, received, product[level], terms, values, level=level,
            )
            received = send(out, below_top)
        else:
            across = first_across <= level + 1 < core
            if not at_home[level]:
                change, out = call(
                    forward_mate, [vec_bf, vec_bf], arrived(received), residue, ahead[level], cost=2
                )
                if joined and level == core - 2:
                    mirror_ends = send(after(ends, out), below_top)
            elif level and not at_home[level - 1]:
                change, out = call(
                    forward_back, [vec_bf, vec_bf], arrived(received), below,
                    product[level - 1], product[level], terms, values, level=level, cost=1,
                )
            elif level == 0 and not at_home[1]:
                change, out, residue = call(
                    forward_first, [vec_bf, vec_bf, vec_bf],
                    residue, received, inverse, coupling, terms, values,
                )
            elif not at_home[level + 1]:
                change, out, residue = call(
                    forward_ahead, [vec_bf, vec_bf, vec_bf],
                    residue, received, product[level], terms, values, level=level,
                )
            else:
                change, out = call(
                    forward, [vec_bf, vec_bf], residue, received, product[level], terms, level=level
                )
            received = send(out, level + 1, across)
            if level == 0 and not joined:
                mirror_gram = send(after(own_gram, out), below_top)
            if not at_home[level]:
                change = mate(change)
            elif not at_home[level + 1]:
                residue = mate(residue)
                ahead[level + 1] = mate(after(ahead[level + 1], out))
            else:
                residue = call(
                    forward_residue, [slab], change, product[level], values, level=level, cost=0
                )
        solved[level] = call(solve, [vec], change, inverse, level=level, cost=6 if level == core - 1 else 1)
    leaf_prod = jnp.einsum("kwn,nm->kwm", leaf_cpl, leaf_inv, preferred_element_type=F32).astype(BF)

    mates = [level for level in range(core) if level % 2 == 0]
    for level in mates:
        product[level] = mate(after(product[level], out))
        solved[level] = mate(after(solved[level], out))
    blocks, mirrored = [None] * levels, [None] * levels
    if joined:
        out_mate = mate(out)
        mirror_pack = after(mirror_pack, out)
        matrices = call(
            join_top, [((2 * width + cols, width), BF)],
            pack, mirror_pack, ends, mirror_ends, inverse, level=core,
        )
        matrices_mate = mate(matrices)
        both, both_bf = ((2, cols, width), F32), ((2, cols, width), BF)
        part, delta = call(join_own, [both, both_bf], out, out_mate, matrices, matrices_mate)
        theirs = mate(received)
        blocks[core], mirrored[core], delta_mirror, block_bf = call(
            join, [vec, vec_bf, ((1, cols, width), BF), vec_bf],
            theirs, received, part, matrices, matrices_mate, solved[core - 1], product[core - 1],
            home=core - 1 not in mates,
        )
        blocks[-1], mirrored[-1] = call(
            top_blocks, [vec, vec_bf], pack, mirror_pack, ends, mirror_ends, delta, delta_mirror
        )
        if core - 1 not in mates:
            blocks[core - 1] = block_bf
        solved_above = core - 1
    else:
        top_pair = call(top_products, [pair], own_gram, mirror_gram, product[-1], cost=8)
        block, block_bf, deltas = call(
            top, [vec, vec_bf, ((2, cols, width), BF)], out, received, top_pair, solved[-1]
        )
        blocks[levels - 2] = block
        received = mirrored[levels - 2] = send(block_bf, levels - 2)
        blocks[-1], mirrored[-1] = call(top_values, [vec, vec_bf], deltas, own_gram, mirror_gram)
        solved_above = levels - 2
    late = [0]
    def pass_on(level, home):
        received = send(block_bf, level, level < core)
        if home == (level < core):
            mirrored[level] = mate(received)
            late.append(level)
        else:
            mirrored[level] = received
        return received

    if joined:
        received = pass_on(solved_above, solved_above not in mates)
    for level in reversed(range(solved_above)):
        home = level not in mates
        outs = [vec, vec_bf] if home else [vec_bf]
        if level + 1 >= core:
            side = 0 if home else 1
            part = call(back_part, [vec], solved[level], block_bf, product[level], side=side)
            made = call(back, outs, part, received, product[level], side=1 - side)
        else:
            known = mate(block_bf)
            if home:
                blocks[level + 1] = known
            made = call(back_both, outs, arrived(received), known, solved[level], product[level])
        if home:
            blocks[level], block_bf = made
        else:
            block_bf = made
        received = pass_on(level, home)
    if 0 in mates:
        blocks[0] = mate(block_bf)
    early = tuple(level for level in range(levels) if level not in late)
    part = call(
        leaf_part, [((cols, size), F32)],
        leaf, leaf_inv, leaf_prod, *[mirrored[level] for level in early], early=early,
    )
    mirrored[0] = arrived(mirrored[0])
    leaf_solution, stacked = call(
        finish, [((cols, size), F32), ((levels, cols, width), F32)],
        part, leaf_prod, *[mirrored[level] for level in late], *blocks, late=tuple(late),
    )
    return leaf_solution.T, jnp.swapaxes(stacked, 1, 2)[None]


def solution(mesh):
    both = ("gx", "gy")
    return jax.shard_map(
        shards,
        mesh=mesh,
        in_specs=tuple(P(both, *[None] * rank) for rank in (1, 2, 3, 3, 3, 5)),
        out_specs=(P(both, None), P(both, None, None, None)),
        check_vma=False,
    )
```

```python
import functools

import jax
import jax.numpy as jnp
from jax import lax
from jax.experimental import pallas as pl
from jax.experimental.pallas import tpu as pltpu
from jax.sharding import PartitionSpec as P

BF = jnp.bfloat16
F32 = jnp.float32
VMEM = pl.BlockSpec(memory_space=pltpu.VMEM)


def times(values, matrix):
    return lax.dot_general(values, matrix, (((1,), (0,)), ((), ())), preferred_element_type=F32)


def times_t(values, matrix):
    return lax.dot_general(values, matrix, (((1,), (1,)), ((), ())), preferred_element_type=F32)


def gram(left, right):
    return lax.dot_general(left, right, (((0,), (0,)), ((), ())), preferred_element_type=F32)


def exchange(value, level, gy_levels, cross=False):
    inner, outer = lax.axis_size("gy"), lax.axis_size("gx")
    mask = 2**level ^ (inner if cross else 0)
    pairs = [(source, source ^ mask) for source in range(inner * outer)]
    return lax.ppermute(value, ("gx", "gy"), pairs)


def call(body, outs, *args, cost=1, **static):
    moved = sum(a.size * a.dtype.itemsize for a in args)
    made = pl.pallas_call(
        functools.partial(body, **static),
        out_shape=[jax.ShapeDtypeStruct(shape, kind) for shape, kind in outs],
        in_specs=[VMEM] * len(args),
        out_specs=[VMEM] * len(outs),
        compiler_params=pltpu.CompilerParams(vmem_limit_bytes=32 * 2**20),
        cost_estimate=pl.CostEstimate(flops=cost * 3 * 10**8, bytes_accessed=moved, transcendentals=0),
    )(*args)
    return made if len(outs) > 1 else made[0]


def products(inverse, coupling, out, *, level):
    for side in range(2):
        out[side] = times(coupling[level, side], inverse[level]).astype(BF)


def products_ahead(inverse, coupling, terms, out, ahead, *, level):
    rows = inverse.shape[1]
    out[0] = times(coupling[level, 0], inverse[level]).astype(BF)
    mirror = times(coupling[level, 1], inverse[level]).astype(BF)
    out[1] = mirror
    ahead[:rows] = mirror
    ahead[rows:] = terms[level + 1].astype(BF)


def top_gram(inverse, out):
    matrix = inverse[inverse.shape[0] - 1]
    out[...] = gram(matrix, matrix).astype(BF)


def top_products(own, mirror, product, out):
    out[0] = times(own[...], product[0]).astype(BF)
    out[1] = times(mirror[...], product[1]).astype(BF)


def forward(residue, received, product, terms, delta, out, *, level):
    change = (residue[0] - received[...].astype(F32)).astype(BF)
    delta[...] = change
    out[...] = (terms[level + 1] + times_t(change, product[1])).astype(BF)


def forward_ahead(residue, received, product, terms, values, delta, out, ahead, *, level):
    change = (residue[0] - received[...].astype(F32)).astype(BF)
    delta[...] = change
    out[...] = (terms[level + 1] + times_t(change, product[1])).astype(BF)
    ahead[...] = (values[level + 1] - times_t(change, product[0])).astype(BF)


def forward_mate(received, residue, ahead, delta, out):
    rows = ahead.shape[1]
    change = (residue[...].astype(F32) - received[...].astype(F32)).astype(BF)
    delta[...] = change
    out[...] = (ahead[rows:].astype(F32) + times_t(change, ahead[:rows])).astype(BF)


def forward_back(received, below, product_below, product, terms, values, delta, out, *, level):
    residue = values[level] - times_t(below[...], product_below[0])
    change = (residue - received[...].astype(F32)).astype(BF)
    delta[...] = change
    out[...] = (terms[level + 1] + times_t(change, product[1])).astype(BF)


def forward_residue(delta, product, values, residue, *, level):
    residue[0] = values[level + 1] - times_t(delta[...], product[0])


def forward_top(residue, received, product, terms, values, delta, out, *, level):
    change = (residue[0] - received[...].astype(F32)).astype(BF)
    delta[...] = change
    rows = change.shape[0]
    out[:rows] = (terms[level + 1] + times_t(change, product[1])).astype(BF)
    out[rows:] = (values[level + 1] - times_t(change, product[0])).astype(BF)


def forward_first(residue, received, inverse, coupling, terms, values, delta, out, ahead):
    change = (residue[0] - received[...].astype(F32)).astype(BF)
    delta[...] = change
    step = times_t(change, inverse[0]).astype(BF)
    out[...] = (terms[1] + times_t(step, coupling[0, 1])).astype(BF)
    ahead[...] = (values[1] - times_t(step, coupling[0, 0])).astype(BF)


def forward_last(received, below, product_below, product, terms, values, delta, out, *, level):
    residue = values[level] - times_t(below[...], product_below[0])
    change = (residue - received[...].astype(F32)).astype(BF)
    delta[...] = change
    rows = change.shape[0]
    out[:rows] = (terms[level + 1] + times_t(change, product[1])).astype(BF)
    out[rows:] = (values[level + 1] - times_t(change, product[0])).astype(BF)


def pack_top(own_gram, inverse, coupling, out, *, level):
    width = inverse.shape[1]
    out[:width] = own_gram[...]
    for side in range(2):
        made = times(coupling[level, side], inverse[level]).astype(BF)
        out[(side + 1) * width : (side + 2) * width] = made


def top_ends(terms, values, out):
    cols = values.shape[1]
    out[:cols] = values[values.shape[0] - 1].astype(BF)
    out[cols:] = terms[terms.shape[0] - 1].astype(BF)


def join_top(mine, mirror, ends, mirror_ends, inverse, sent, out, *, level):
    width = inverse.shape[1]
    gram_mine, gram_mirror = mine[:width], mirror[:width]
    own, other = mine[width : 2 * width], mine[2 * width : 3 * width]
    mirror_own, mirror_other = mirror[width : 2 * width], mirror[2 * width : 3 * width]
    first = times(gram_mine, own).astype(BF)
    second = times(gram_mirror, other).astype(BF)
    matrix = inverse[level]
    out[:width] = (gram(matrix, matrix) + gram(own, first) + gram(other, second)).astype(BF)
    out[width : 2 * width] = (gram(mirror_other, first) + gram(mirror_own, second)).astype(BF)
    right, mirror_right = top_rights(ends, mirror_ends)
    cols = right.shape[0]
    out[2 * width : 2 * width + cols] = (-times(right, first) - times(mirror_right, second)).astype(BF)
    out[2 * width + cols :] = sent[...]


def top_rights(mine, mirror):
    cols = mine.shape[0] // 2
    right = mine[:cols].astype(F32) - mirror[cols:].astype(F32)
    mirror_right = mirror[:cols].astype(F32) - mine[cols:].astype(F32)
    return right.astype(BF), mirror_right.astype(BF)


def join_own(joined, joined_mate, out, delta):
    rows, width = out.shape[1], joined.shape[1]
    mine, mate = joined[2 * width + rows :], joined_mate[2 * width + rows :]
    for at, (a, b, matrices) in enumerate(((mine, mate, joined), (mate, mine, joined_mate))):
        change = (a[rows:].astype(F32) - b[:rows].astype(F32)).astype(BF)
        delta[at] = change
        out[at] = times(change, matrices[:width]) + matrices[2 * width : 2 * width + rows].astype(F32)


def join(theirs, across, part, joined, joined_mate, solved, product, block, block_mate, delta, below, *, home):
    rows, width = part.shape[1], joined.shape[1]
    found = []
    pairs = ((theirs, across, joined), (across, theirs, joined_mate))
    for at, (a, b, matrices) in enumerate(pairs):
        change = (a[rows:].astype(F32) - b[:rows].astype(F32)).astype(BF)
        value = part[at] + times(change, matrices[width : 2 * width])
        found.append(value.astype(BF))
        if at == 0:
            block[...] = value
            delta[0] = change
    block_mate[...] = found[1]
    own, other = found if home else found[::-1]
    below[...] = (solved[...] - times(own, product[0]) - times(other, product[1])).astype(BF)


def top_blocks(mine, mirror, ends, mirror_ends, delta, delta_mirror, out, mirrored):
    width = out.shape[1]
    right, mirror_right = top_rights(ends, mirror_ends)
    change, other = delta[0], delta_mirror[0]
    own = right.astype(F32) - times_t(change, mine[width : 2 * width])
    own = own - times_t(other, mirror[2 * width : 3 * width])
    theirs = mirror_right.astype(F32) - times_t(other, mirror[width : 2 * width])
    theirs = theirs - times_t(change, mine[2 * width : 3 * width])
    out[...] = times(own.astype(BF), mine[:width])
    mirrored[...] = times(theirs.astype(BF), mirror[:width]).astype(BF)


def solve(delta, inverse, solved, *, level):
    step = times_t(delta[...], inverse[level]).astype(BF)
    solved[...] = times(step, inverse[level])


def top(mine, received, product, solved, out, out_bf, delta):
    rows = solved.shape[0]
    own = (mine[rows:].astype(F32) - received[:rows].astype(F32)).astype(BF)
    other = (received[rows:].astype(F32) - mine[:rows].astype(F32)).astype(BF)
    value = solved[...] - times(own, product[0]) - times(other, product[1])
    out[...] = value
    out_bf[...] = value.astype(BF)
    delta[0] = own
    delta[1] = other


def top_values(delta, own, mirror, out, mirrored):
    out[...] = times(delta[0], own[...])
    mirrored[...] = times(delta[1], mirror[...]).astype(BF)


def back_part(solved, known, product, out, *, side):
    out[...] = solved[...] - times(known[...].astype(BF), product[side])


def back(part, received, product, *outs, side):
    value = part[...] - times(received[...].astype(BF), product[side])
    for out in outs:
        out[...] = value.astype(out.dtype)


def back_both(received, known, solved, product, *outs):
    value = solved[...] - times(known[...], product[0])
    value = value - times(received[...].astype(BF), product[1])
    for out in outs:
        out[...] = value.astype(out.dtype)


def leaf_part(leaf, inverse, leaf_products, *refs, early):
    *mirrored, out = refs
    total = times(leaf[...].astype(BF), inverse[...])
    for level, block in zip(early, mirrored, strict=True):
        total = total - times(block[...], leaf_products[level])
    out[...] = total


def finish(part, leaf_products, *refs, late):
    *refs, leaf, out = refs
    mirrored, blocks = refs[: len(late)], refs[len(late) :]
    total = part[...]
    for level, block in zip(late, mirrored, strict=True):
        total = total - times(block[...].astype(BF), leaf_products[level])
    leaf[...] = total
    for level, block in enumerate(blocks):
        out[level] = block[...].astype(F32)


def shards(leaf_values, leaf_inverse, leaf_coupling, block_values, block_inverse, block_coupling):
    levels, width = block_inverse.shape[1], block_inverse.shape[2]
    size, cols = leaf_values.shape
    core = lax.axis_size("gy").bit_length() - 1
    inverse, coupling = block_inverse[0], block_coupling[0, :, 0]
    leaf_inv, leaf_cpl = leaf_inverse[0], leaf_coupling[0]
    values = jnp.swapaxes(block_values[0], 1, 2)
    vec, vec_bf, pair = ((cols, width), F32), ((cols, width), BF), ((2, width, width), BF)
    slab = ((1, cols, width), F32)

    def send(value, level, cross=False):
        return exchange(value, level, core, cross)

    def mate(value):
        return exchange(value, core, core)

    def arrived(value):
        return value.astype(F32)

    def after(value, other):
        return lax.optimization_barrier((value, other))[0]

    below_top = levels - 1
    first_across = 1 + (core - 1) % 2
    at_home = [
        level < first_across or level >= core or (level - first_across) % 2 == 1
        for level in range(levels)
    ]
    leaf = times_t(leaf_values.T.astype(BF), leaf_inv)
    terms = jnp.einsum("kwn,rn->krw", leaf_cpl, leaf.astype(BF), preferred_element_type=F32)
    received = send(terms[0].astype(BF), 0)
    product, ahead, solved = [None] * below_top, [None] * below_top, [None] * below_top
    joined = levels == core + 2 and core >= 3
    own_gram = call(top_gram, [((width, width), BF)], inverse)
    inverse_later = after(inverse, own_gram)
    if joined:
        pack = call(
            pack_top, [((3 * width, width), BF)], own_gram, inverse_later, coupling, level=core
        )
        mirror_pack = send(pack, below_top)
        inverse_later = after(inverse, pack)
        ends = call(top_ends, [((2 * cols, width), BF)], terms, values)
    for level in range(core if joined else below_top):
        if at_home[level]:
            product[level] = call(products, [pair], inverse_later, coupling, level=level, cost=(8, 1, 1)[min(level, 2)])
        else:
            product[level], ahead[level] = call(
                products_ahead, [pair, ((width + cols, width), BF)],
                inverse_later, coupling, terms, level=level,
            )

    residue, change = values, None
    for level in range(core if joined else below_top):
        below = change
        if joined and level == core - 1:
            change, out = call(
                forward_last, [vec_bf, ((2 * cols, width), BF)], arrived(received), below,
                product[level - 1], product[level], terms, values, level=level, cost=4,
            )
            received = send(out, below_top, True)
        elif level == levels - 2:
            received, mirror_gram = lax.optimization_barrier((received, mirror_gram))
            change, out = call(
                forward_top, [vec_bf, ((2 * cols, width), BF)],
                residue, received, product[level], terms, values, level=level,
            )
            received = send(out, below_top)
        else:
            across = first_across <= level + 1 < core
            if not at_home[level]:
                if joined and level == core - 2:
                    sent, product[level + 1], ends = lax.optimization_barrier(
                        (ahead[level], product[level + 1], ends)
                    )
                    ahead[level] = sent
                change, out = call(
                    forward_mate, [vec_bf, vec_bf], arrived(received), residue, ahead[level], cost=2
                )
                if joined and level == core - 2:
                    mirror_ends = send(after(ends, out), below_top)
            elif level and not at_home[level - 1]:
                change, out = call(
                    forward_back, [vec_bf, vec_bf], arrived(received), below,
                    product[level - 1], product[level], terms, values, level=level, cost=1,
                )
            elif level == 0 and not at_home[1]:
                change, out, residue = call(
                    forward_first, [vec_bf, vec_bf, vec_bf],
                    residue, received, inverse, coupling, terms, values,
                )
            elif not at_home[level + 1]:
                change, out, residue = call(
                    forward_ahead, [vec_bf, vec_bf, vec_bf],
                    residue, received, product[level], terms, values, level=level,
                )
            else:
                change, out = call(
                    forward, [vec_bf, vec_bf], residue, received, product[level], terms, level=level
                )
            received = send(out, level + 1, across)
            if level == 0 and not joined:
                mirror_gram = send(after(own_gram, out), below_top)
            if not at_home[level]:
                change = mate(change)
            elif not at_home[level + 1]:
                residue = mate(residue)
                ahead[level + 1] = mate(after(ahead[level + 1], out))
            else:
                residue = call(
                    forward_residue, [slab], change, product[level], values, level=level, cost=0
                )
        solved[level] = call(solve, [vec], change, inverse, level=level, cost=8 if level == core - 1 else 1)
    leaf_prod = jnp.einsum("kwn,nm->kwm", leaf_cpl, leaf_inv, preferred_element_type=F32).astype(BF)

    mates = [level for level in range(core) if level % 2 == 0]
    for level in mates:
        product[level] = mate(after(product[level], out))
        solved[level] = mate(after(solved[level], out))
    blocks, mirrored = [None] * levels, [None] * levels
    if joined:
        mirror_pack = after(mirror_pack, out)
        matrices = call(
            join_top, [((2 * width + 3 * cols, width), BF)],
            pack, mirror_pack, ends, mirror_ends, inverse, out, level=core, cost=1,
        )
        matrices_mate = mate(matrices)
        both, both_bf = ((2, cols, width), F32), ((2, cols, width), BF)
        part, delta = call(join_own, [both, both_bf], matrices, matrices_mate)
        theirs = mate(received)
        blocks[core], mirrored[core], delta_mirror, block_bf = call(
            join, [vec, vec_bf, ((1, cols, width), BF), vec_bf],
            theirs, received, part, matrices, matrices_mate, solved[core - 1], product[core - 1],
            home=core - 1 not in mates,
        )
        blocks[-1], mirrored[-1] = call(
            top_blocks, [vec, vec_bf], pack, mirror_pack, ends, mirror_ends, delta, delta_mirror
        )
        if core - 1 not in mates:
            blocks[core - 1] = block_bf
        solved_above = core - 1
    else:
        top_pair = call(top_products, [pair], own_gram, mirror_gram, product[-1], cost=8)
        block, block_bf, deltas = call(
            top, [vec, vec_bf, ((2, cols, width), BF)], out, received, top_pair, solved[-1]
        )
        blocks[levels - 2] = block
        received = mirrored[levels - 2] = send(block_bf, levels - 2)
        blocks[-1], mirrored[-1] = call(top_values, [vec, vec_bf], deltas, own_gram, mirror_gram)
        solved_above = levels - 2
    late = [0]
    def pass_on(level, home):
        received = send(block_bf, level, level < core)
        if home == (level < core):
            mirrored[level] = mate(received)
            late.append(level)
        else:
            mirrored[level] = received
        return received

    if joined:
        received = pass_on(solved_above, solved_above not in mates)
    for level in reversed(range(solved_above)):
        home = level not in mates
        outs = [vec, vec_bf] if home else [vec_bf]
        if level + 1 >= core:
            side = 0 if home else 1
            part = call(back_part, [vec], solved[level], block_bf, product[level], side=side)
            made = call(back, outs, part, received, product[level], side=1 - side)
        else:
            known = mate(block_bf)
            if home:
                blocks[level + 1] = known
            made = call(back_both, outs, arrived(received), known, solved[level], product[level])
        if home:
            blocks[level], block_bf = made
        else:
            block_bf = made
        received = pass_on(level, home)
    if 0 in mates:
        blocks[0] = mate(block_bf)
    early = tuple(level for level in range(levels) if level not in late)
    part = call(
        leaf_part, [((cols, size), F32)],
        leaf, leaf_inv, leaf_prod, *[mirrored[level] for level in early], early=early,
    )
    mirrored[0] = arrived(mirrored[0])
    leaf_solution, stacked = call(
        finish, [((cols, size), F32), ((levels, cols, width), F32)],
        part, leaf_prod, *[mirrored[level] for level in late], *blocks, late=tuple(late),
    )
    return leaf_solution.T, jnp.swapaxes(stacked, 1, 2)[None]


def solution(mesh):
    both = ("gx", "gy")
    return jax.shard_map(
        shards,
        mesh=mesh,
        in_specs=tuple(P(both, *[None] * rank) for rank in (1, 2, 3, 3, 3, 5)),
        out_specs=(P(both, None), P(both, None, None, None)),
        check_vma=False,
    )
```

```python
import functools

import jax
import jax.numpy as jnp
from jax import lax
from jax.experimental import pallas as pl
from jax.experimental.pallas import tpu as pltpu
from jax.sharding import PartitionSpec as P

BF = jnp.bfloat16
F32 = jnp.float32
VMEM = pl.BlockSpec(memory_space=pltpu.VMEM)


def times(values, matrix):
    return lax.dot_general(values, matrix, (((1,), (0,)), ((), ())), preferred_element_type=F32)


def times_t(values, matrix):
    return lax.dot_general(values, matrix, (((1,), (1,)), ((), ())), preferred_element_type=F32)


def gram(left, right):
    return lax.dot_general(left, right, (((0,), (0,)), ((), ())), preferred_element_type=F32)


def exchange(value, level, gy_levels, cross=False):
    inner, outer = lax.axis_size("gy"), lax.axis_size("gx")
    mask = 2**level ^ (inner if cross else 0)
    pairs = [(source, source ^ mask) for source in range(inner * outer)]
    return lax.ppermute(value, ("gx", "gy"), pairs)


def call(body, outs, *args, cost=1, **static):
    moved = sum(a.size * a.dtype.itemsize for a in args)
    made = pl.pallas_call(
        functools.partial(body, **static),
        out_shape=[jax.ShapeDtypeStruct(shape, kind) for shape, kind in outs],
        in_specs=[VMEM] * len(args),
        out_specs=[VMEM] * len(outs),
        compiler_params=pltpu.CompilerParams(vmem_limit_bytes=32 * 2**20),
        cost_estimate=pl.CostEstimate(flops=cost * 3 * 10**8, bytes_accessed=moved, transcendentals=0),
    )(*args)
    return made if len(outs) > 1 else made[0]


def products(inverse, coupling, out, *, level):
    for side in range(2):
        out[side] = times(coupling[level, side], inverse[level]).astype(BF)


def products_ahead(inverse, coupling, terms, out, ahead, *, level):
    rows = inverse.shape[1]
    out[0] = times(coupling[level, 0], inverse[level]).astype(BF)
    mirror = times(coupling[level, 1], inverse[level]).astype(BF)
    out[1] = mirror
    ahead[:rows] = mirror
    ahead[rows:] = terms[level + 1].astype(BF)


def top_gram(inverse, out):
    matrix = inverse[inverse.shape[0] - 1]
    out[...] = gram(matrix, matrix).astype(BF)


def top_products(own, mirror, product, out):
    out[0] = times(own[...], product[0]).astype(BF)
    out[1] = times(mirror[...], product[1]).astype(BF)


def forward(residue, received, product, terms, delta, out, *, level):
    change = (residue[0] - received[...].astype(F32)).astype(BF)
    delta[...] = change
    out[...] = (terms[level + 1] + times_t(change, product[1])).astype(BF)


def forward_ahead(residue, received, product, terms, values, delta, out, ahead, *, level):
    change = (residue[0] - received[...].astype(F32)).astype(BF)
    delta[...] = change
    out[...] = (terms[level + 1] + times_t(change, product[1])).astype(BF)
    ahead[...] = (values[level + 1] - times_t(change, product[0])).astype(BF)


def forward_mate(received, residue, ahead, delta, out):
    rows = ahead.shape[1]
    change = (residue[...].astype(F32) - received[...].astype(F32)).astype(BF)
    delta[...] = change
    out[...] = (ahead[rows:].astype(F32) + times_t(change, ahead[:rows])).astype(BF)


def forward_back(received, below, product_below, product, terms, values, delta, out, *, level):
    residue = values[level] - times_t(below[...], product_below[0])
    change = (residue - received[...].astype(F32)).astype(BF)
    delta[...] = change
    out[...] = (terms[level + 1] + times_t(change, product[1])).astype(BF)


def forward_residue(delta, product, values, residue, *, level):
    residue[0] = values[level + 1] - times_t(delta[...], product[0])


def forward_top(residue, received, product, terms, values, delta, out, *, level):
    change = (residue[0] - received[...].astype(F32)).astype(BF)
    delta[...] = change
    rows = change.shape[0]
    out[:rows] = (terms[level + 1] + times_t(change, product[1])).astype(BF)
    out[rows:] = (values[level + 1] - times_t(change, product[0])).astype(BF)


def forward_first(residue, received, inverse, coupling, terms, values, delta, out, ahead):
    change = (residue[0] - received[...].astype(F32)).astype(BF)
    delta[...] = change
    step = times_t(change, inverse[0]).astype(BF)
    out[...] = (terms[1] + times_t(step, coupling[0, 1])).astype(BF)
    ahead[...] = (values[1] - times_t(step, coupling[0, 0])).astype(BF)


def forward_last(received, below, product_below, product, terms, values, delta, out, *, level):
    residue = values[level] - times_t(below[...], product_below[0])
    change = (residue - received[...].astype(F32)).astype(BF)
    delta[...] = change
    rows = change.shape[0]
    out[:rows] = (terms[level + 1] + times_t(change, product[1])).astype(BF)
    out[rows:] = (values[level + 1] - times_t(change, product[0])).astype(BF)


def pack_top(inverse, coupling, out, *, level):
    width = inverse.shape[1]
    for side in range(2):
        made = times(coupling[level, side], inverse[level]).astype(BF)
        out[side * width : (side + 1) * width] = made


def top_ends(own_gram, terms, values, out):
    width, cols = own_gram.shape[0], values.shape[1]
    out[:width] = own_gram[...]
    out[width : width + cols] = values[values.shape[0] - 1].astype(BF)
    out[width + cols :] = terms[terms.shape[0] - 1].astype(BF)


def join_top(mine, mirror, ends, mirror_ends, inverse, sent, out, *, level):
    width = inverse.shape[1]
    gram_mine, gram_mirror = ends[:width], mirror_ends[:width]
    own, other = mine[:width], mine[width:]
    mirror_own, mirror_other = mirror[:width], mirror[width:]
    first = times(gram_mine, own).astype(BF)
    second = times(gram_mirror, other).astype(BF)
    matrix = inverse[level]
    out[:width] = (gram(matrix, matrix) + gram(own, first) + gram(other, second)).astype(BF)
    out[width : 2 * width] = (gram(mirror_other, first) + gram(mirror_own, second)).astype(BF)
    right, mirror_right = top_rights(ends, mirror_ends)
    cols = right.shape[0]
    out[2 * width : 2 * width + cols] = (-times(right, first) - times(mirror_right, second)).astype(BF)
    out[2 * width + cols :] = sent[...]


def top_rights(mine, mirror):
    width = mine.shape[1]
    cols = (mine.shape[0] - width) // 2
    right = mine[width : width + cols].astype(F32) - mirror[width + cols :].astype(F32)
    mirror_right = mirror[width : width + cols].astype(F32) - mine[width + cols :].astype(F32)
    return right.astype(BF), mirror_right.astype(BF)


def join_own(joined, joined_mate, out, delta):
    rows, width = out.shape[1], joined.shape[1]
    mine, mate = joined[2 * width + rows :], joined_mate[2 * width + rows :]
    for at, (a, b, matrices) in enumerate(((mine, mate, joined), (mate, mine, joined_mate))):
        change = (a[rows:].astype(F32) - b[:rows].astype(F32)).astype(BF)
        delta[at] = change
        out[at] = times(change, matrices[:width]) + matrices[2 * width : 2 * width + rows].astype(F32)


def join(theirs, across, part, joined, joined_mate, solved, product, block, block_mate, delta, below, *, home):
    rows, width = part.shape[1], joined.shape[1]
    found = []
    pairs = ((theirs, across, joined), (across, theirs, joined_mate))
    for at, (a, b, matrices) in enumerate(pairs):
        change = (a[rows:].astype(F32) - b[:rows].astype(F32)).astype(BF)
        value = part[at] + times(change, matrices[width : 2 * width])
        found.append(value.astype(BF))
        if at == 0:
            block[...] = value
            delta[0] = change
    block_mate[...] = found[1]
    own, other = found if home else found[::-1]
    below[...] = (solved[...] - times(own, product[0]) - times(other, product[1])).astype(BF)


def top_blocks(mine, mirror, ends, mirror_ends, delta, delta_mirror, out, mirrored):
    width = out.shape[1]
    right, mirror_right = top_rights(ends, mirror_ends)
    change, other = delta[0], delta_mirror[0]
    own = right.astype(F32) - times_t(change, mine[:width])
    own = own - times_t(other, mirror[width:])
    theirs = mirror_right.astype(F32) - times_t(other, mirror[:width])
    theirs = theirs - times_t(change, mine[width:])
    out[...] = times(own.astype(BF), ends[:width])
    mirrored[...] = times(theirs.astype(BF), mirror_ends[:width]).astype(BF)


def solve(delta, inverse, solved, *, level):
    step = times_t(delta[...], inverse[level]).astype(BF)
    solved[...] = times(step, inverse[level])


def top(mine, received, product, solved, out, out_bf, delta):
    rows = solved.shape[0]
    own = (mine[rows:].astype(F32) - received[:rows].astype(F32)).astype(BF)
    other = (received[rows:].astype(F32) - mine[:rows].astype(F32)).astype(BF)
    value = solved[...] - times(own, product[0]) - times(other, product[1])
    out[...] = value
    out_bf[...] = value.astype(BF)
    delta[0] = own
    delta[1] = other


def top_values(delta, own, mirror, out, mirrored):
    out[...] = times(delta[0], own[...])
    mirrored[...] = times(delta[1], mirror[...]).astype(BF)


def back_part(solved, known, product, out, *, side):
    out[...] = solved[...] - times(known[...].astype(BF), product[side])


def back(part, received, product, *outs, side):
    value = part[...] - times(received[...].astype(BF), product[side])
    for out in outs:
        out[...] = value.astype(out.dtype)


def back_both(received, known, solved, product, *outs):
    value = solved[...] - times(known[...], product[0])
    value = value - times(received[...].astype(BF), product[1])
    for out in outs:
        out[...] = value.astype(out.dtype)


def leaf_part(leaf, inverse, leaf_products, *refs, early):
    *mirrored, out = refs
    total = times(leaf[...].astype(BF), inverse[...])
    for level, block in zip(early, mirrored, strict=True):
        total = total - times(block[...], leaf_products[level])
    out[...] = total


def finish(part, leaf_products, *refs, late):
    *refs, leaf, out = refs
    mirrored, blocks = refs[: len(late)], refs[len(late) :]
    total = part[...]
    for level, block in zip(late, mirrored, strict=True):
        total = total - times(block[...].astype(BF), leaf_products[level])
    leaf[...] = total
    for level, block in enumerate(blocks):
        out[level] = block[...].astype(F32)


def shards(leaf_values, leaf_inverse, leaf_coupling, block_values, block_inverse, block_coupling):
    levels, width = block_inverse.shape[1], block_inverse.shape[2]
    size, cols = leaf_values.shape
    core = lax.axis_size("gy").bit_length() - 1
    inverse, coupling = block_inverse[0], block_coupling[0, :, 0]
    leaf_inv, leaf_cpl = leaf_inverse[0], leaf_coupling[0]
    values = jnp.swapaxes(block_values[0], 1, 2)
    vec, vec_bf, pair = ((cols, width), F32), ((cols, width), BF), ((2, width, width), BF)
    slab = ((1, cols, width), F32)

    def send(value, level, cross=False):
        return exchange(value, level, core, cross)

    def mate(value):
        return exchange(value, core, core)

    def arrived(value):
        return value.astype(F32)

    def after(value, other):
        return lax.optimization_barrier((value, other))[0]

    below_top = levels - 1
    first_across = 1 + (core - 1) % 2
    at_home = [
        level < first_across or level >= core or (level - first_across) % 2 == 1
        for level in range(levels)
    ]
    leaf = times_t(leaf_values.T.astype(BF), leaf_inv)
    terms = jnp.einsum("kwn,rn->krw", leaf_cpl, leaf.astype(BF), preferred_element_type=F32)
    received = send(terms[0].astype(BF), 0)
    product, ahead, solved = [None] * below_top, [None] * below_top, [None] * below_top
    joined = levels == core + 2 and core >= 3
    own_gram = call(top_gram, [((width, width), BF)], inverse)
    inverse_later = after(inverse, own_gram)
    if joined:
        pack = call(
            pack_top, [((2 * width, width), BF)], inverse_later, coupling, level=core
        )
        mirror_pack = send(pack, below_top)
        inverse_later = after(inverse, pack)
        ends = call(top_ends, [((width + 2 * cols, width), BF)], own_gram, terms, values, cost=0)
    for level in range(core if joined else below_top):
        if at_home[level]:
            product[level] = call(products, [pair], inverse_later, coupling, level=level, cost=(8, 1, 1)[min(level, 2)])
        else:
            product[level], ahead[level] = call(
                products_ahead, [pair, ((width + cols, width), BF)],
                inverse_later, coupling, terms, level=level,
            )

    residue, change = values, None
    for level in range(core if joined else below_top):
        below = change
        if joined and level == core - 1:
            below, mirror_pack = lax.optimization_barrier((below, mirror_pack))
            change, out = call(
                forward_last, [vec_bf, ((2 * cols, width), BF)], arrived(received), below,
                product[level - 1], product[level], terms, values, level=level, cost=4,
            )
            received = send(out, below_top, True)
        elif level == levels - 2:
            received, mirror_gram = lax.optimization_barrier((received, mirror_gram))
            change, out = call(
                forward_top, [vec_bf, ((2 * cols, width), BF)],
                residue, received, product[level], terms, values, level=level,
            )
            received = send(out, below_top)
        else:
            across = first_across <= level + 1 < core
            if not at_home[level]:
                if joined and level == core - 2:
                    ahead[level], ends = lax.optimization_barrier((ahead[level], ends))
                change, out = call(
                    forward_mate, [vec_bf, vec_bf], arrived(received), residue, ahead[level], cost=2
                )
            elif level and not at_home[level - 1]:
                change, out = call(
                    forward_back, [vec_bf, vec_bf], arrived(received), below,
                    product[level - 1], product[level], terms, values, level=level, cost=1,
                )
            elif level == 0 and not at_home[1]:
                change, out, residue = call(
                    forward_first, [vec_bf, vec_bf, vec_bf],
                    residue, received, inverse, coupling, terms, values, cost=0,
                )
            elif not at_home[level + 1]:
                change, out, residue = call(
                    forward_ahead, [vec_bf, vec_bf, vec_bf],
                    residue, received, product[level], terms, values, level=level,
                )
            else:
                change, out = call(
                    forward, [vec_bf, vec_bf], residue, received, product[level], terms, level=level
                )
            received = send(out, level + 1, across)
            if level == 0:
                if joined:
                    mirror_ends = send(after(ends, out), below_top)
                else:
                    mirror_gram = send(after(own_gram, out), below_top)
            if not at_home[level]:
                change = mate(change)
            elif not at_home[level + 1]:
                residue = mate(residue)
                ahead[level + 1] = mate(after(ahead[level + 1], out))
            else:
                residue = call(
                    forward_residue, [slab], change, product[level], values, level=level, cost=0
                )
        solved[level] = call(solve, [vec], change, inverse, level=level, cost=8 if level == core - 1 else 1)
    leaf_prod = jnp.einsum("kwn,nm->kwm", leaf_cpl, leaf_inv, preferred_element_type=F32).astype(BF)

    mates = [level for level in range(core) if level % 2 == 0]
    for level in mates:
        product[level] = mate(after(product[level], out))
        solved[level] = mate(after(solved[level], out))
    blocks, mirrored = [None] * levels, [None] * levels
    if joined:
        mirror_ends = after(mirror_ends, out)
        matrices = call(
            join_top, [((2 * width + 3 * cols, width), BF)],
            pack, mirror_pack, ends, mirror_ends, inverse, out, level=core, cost=1,
        )
        matrices_mate = mate(matrices)
        both, both_bf = ((2, cols, width), F32), ((2, cols, width), BF)
        part, delta = call(join_own, [both, both_bf], matrices, matrices_mate)
        theirs = mate(received)
        blocks[core], mirrored[core], delta_mirror, block_bf = call(
            join, [vec, vec_bf, ((1, cols, width), BF), vec_bf],
            theirs, received, part, matrices, matrices_mate, solved[core - 1], product[core - 1],
            home=core - 1 not in mates,
        )
        blocks[-1], mirrored[-1] = call(
            top_blocks, [vec, vec_bf], pack, mirror_pack, ends, mirror_ends, delta, delta_mirror
        )
        if core - 1 not in mates:
            blocks[core - 1] = block_bf
        solved_above = core - 1
    else:
        top_pair = call(top_products, [pair], own_gram, mirror_gram, product[-1], cost=8)
        block, block_bf, deltas = call(
            top, [vec, vec_bf, ((2, cols, width), BF)], out, received, top_pair, solved[-1]
        )
        blocks[levels - 2] = block
        received = mirrored[levels - 2] = send(block_bf, levels - 2)
        blocks[-1], mirrored[-1] = call(top_values, [vec, vec_bf], deltas, own_gram, mirror_gram)
        solved_above = levels - 2
    late = [0]
    def pass_on(level, home):
        received = send(block_bf, level, level < core)
        if home == (level < core):
            mirrored[level] = mate(received)
            late.append(level)
        else:
            mirrored[level] = received
        return received

    if joined:
        received = pass_on(solved_above, solved_above not in mates)
    for level in reversed(range(solved_above)):
        home = level not in mates
        outs = [vec, vec_bf] if home else [vec_bf]
        if level + 1 >= core:
            side = 0 if home else 1
            part = call(back_part, [vec], solved[level], block_bf, product[level], side=side)
            made = call(back, outs, part, received, product[level], side=1 - side)
        else:
            known = mate(block_bf)
            if home:
                blocks[level + 1] = known
            made = call(back_both, outs, arrived(received), known, solved[level], product[level])
        if home:
            blocks[level], block_bf = made
        else:
            block_bf = made
        received = pass_on(level, home)
    if 0 in mates:
        blocks[0] = mate(block_bf)
    early = tuple(level for level in range(levels) if level not in late)
    part = call(
        leaf_part, [((cols, size), F32)],
        leaf, leaf_inv, leaf_prod, *[mirrored[level] for level in early], early=early,
    )
    mirrored[0] = arrived(mirrored[0])
    leaf_solution, stacked = call(
        finish, [((cols, size), F32), ((levels, cols, width), F32)],
        part, leaf_prod, *[mirrored[level] for level in late], *blocks, late=tuple(late),
    )
    return leaf_solution.T, jnp.swapaxes(stacked, 1, 2)[None]


def solution(mesh):
    both = ("gx", "gy")
    return jax.shard_map(
        shards,
        mesh=mesh,
        in_specs=tuple(P(both, *[None] * rank) for rank in (1, 2, 3, 3, 3, 5)),
        out_specs=(P(both, None), P(both, None, None, None)),
        check_vma=False,
    )
```

```python
import functools

import jax
import jax.numpy as jnp
from jax import lax
from jax.experimental import pallas as pl
from jax.experimental.pallas import tpu as pltpu
from jax.sharding import PartitionSpec as P

BF = jnp.bfloat16
F32 = jnp.float32
VMEM = pl.BlockSpec(memory_space=pltpu.VMEM)


def times(values, matrix):
    return lax.dot_general(values, matrix, (((1,), (0,)), ((), ())), preferred_element_type=F32)


def times_t(values, matrix):
    return lax.dot_general(values, matrix, (((1,), (1,)), ((), ())), preferred_element_type=F32)


def gram(left, right):
    return lax.dot_general(left, right, (((0,), (0,)), ((), ())), preferred_element_type=F32)


def turned(inverse, coupling):
    return lax.dot_general(inverse, coupling, (((0,), (1,)), ((), ())), preferred_element_type=F32)


def exchange(value, level, gy_levels, cross=False):
    inner, outer = lax.axis_size("gy"), lax.axis_size("gx")
    mask = 2**level ^ (inner if cross else 0)
    pairs = [(source, source ^ mask) for source in range(inner * outer)]
    return lax.ppermute(value, ("gx", "gy"), pairs)


def call(body, outs, *args, cost=1, **static):
    moved = sum(a.size * a.dtype.itemsize for a in args)
    made = pl.pallas_call(
        functools.partial(body, **static),
        out_shape=[jax.ShapeDtypeStruct(shape, kind) for shape, kind in outs],
        in_specs=[VMEM] * len(args),
        out_specs=[VMEM] * len(outs),
        compiler_params=pltpu.CompilerParams(vmem_limit_bytes=32 * 2**20),
        cost_estimate=pl.CostEstimate(flops=cost * 3 * 10**8, bytes_accessed=moved, transcendentals=0),
    )(*args)
    return made if len(outs) > 1 else made[0]


def products(inverse, coupling, out, *, level):
    for side in range(2):
        out[side] = times(coupling[level, side], inverse[level]).astype(BF)


def products_ahead(inverse, coupling, terms, ahead, *, level):
    rows = inverse.shape[1]
    ahead[:rows] = turned(inverse[level], coupling[level, 1]).astype(BF)
    ahead[rows:] = terms[level + 1].astype(BF)


def products_last(inverse, coupling, out, out_turned, below, below_turned, *, level):
    for side in range(2):
        out[side] = times(coupling[level, side], inverse[level]).astype(BF)
        below[side] = times(coupling[level - 1, side], inverse[level - 1]).astype(BF)
        out_turned[side] = turned(inverse[level], coupling[level, side]).astype(BF)
    below_turned[...] = turned(inverse[level - 1], coupling[level - 1, 0]).astype(BF)


def top_gram(inverse, out):
    matrix = inverse[inverse.shape[0] - 1]
    out[...] = gram(matrix, matrix).astype(BF)


def top_products(own, mirror, product, out):
    out[0] = times(own[...], product[0]).astype(BF)
    out[1] = times(mirror[...], product[1]).astype(BF)


def forward(residue, received, product, terms, delta, out, *, level):
    change = (residue[0] - received[...].astype(F32)).astype(BF)
    delta[...] = change
    out[...] = (terms[level + 1] + times_t(change, product[1])).astype(BF)


def forward_ahead(residue, received, product, terms, values, delta, out, ahead, *, level):
    change = (residue[0] - received[...].astype(F32)).astype(BF)
    delta[...] = change
    out[...] = (terms[level + 1] + times_t(change, product[1])).astype(BF)
    ahead[...] = (values[level + 1] - times_t(change, product[0])).astype(BF)


def forward_mate(received, residue, ahead, delta, out):
    rows = ahead.shape[1]
    change = (residue[...].astype(F32) - received[...].astype(F32)).astype(BF)
    delta[...] = change
    out[...] = (ahead[rows:].astype(F32) + times(change, ahead[:rows])).astype(BF)


def forward_back(received, below, product_below, product, terms, values, delta, out, *, level):
    residue = values[level] - times_t(below[...], product_below[0])
    change = (residue - received[...].astype(F32)).astype(BF)
    delta[...] = change
    out[...] = (terms[level + 1] + times_t(change, product[1])).astype(BF)


def forward_residue(delta, product, values, residue, *, level):
    residue[0] = values[level + 1] - times_t(delta[...], product[0])


def forward_top(residue, received, product, terms, values, delta, out, *, level):
    change = (residue[0] - received[...].astype(F32)).astype(BF)
    delta[...] = change
    rows = change.shape[0]
    out[:rows] = (terms[level + 1] + times_t(change, product[1])).astype(BF)
    out[rows:] = (values[level + 1] - times_t(change, product[0])).astype(BF)


def forward_lowest(residue, received, product, terms, values, delta, out, ahead):
    change = (residue[0] - received[...].astype(F32)).astype(BF)
    delta[...] = change
    out[...] = (terms[1] + times(change, product[1])).astype(BF)
    ahead[...] = (values[1] - times(change, product[0])).astype(BF)


def forward_last(received, below, product_below, product, terms, values, delta, out, *, level):
    residue = values[level] - times(below[...], product_below[...])
    change = (residue - received[...].astype(F32)).astype(BF)
    delta[...] = change
    rows = change.shape[0]
    out[:rows] = (terms[level + 1] + times(change, product[1])).astype(BF)
    out[rows:] = (values[level + 1] - times(change, product[0])).astype(BF)


def early_products(inverse, coupling, terms, pack, ahead, lowest, *, level):
    width = inverse.shape[1]
    for side in range(2):
        made = times(coupling[level, side], inverse[level]).astype(BF)
        pack[side * width : (side + 1) * width] = made
        lowest[side] = turned(inverse[0], coupling[0, side]).astype(BF)
    products_ahead(inverse, coupling, terms, ahead, level=1)


def top_ends(own_gram, terms, values, out):
    width, cols = own_gram.shape[0], values.shape[1]
    out[:width] = own_gram[...]
    out[width : width + cols] = values[values.shape[0] - 1].astype(BF)
    out[width + cols :] = terms[terms.shape[0] - 1].astype(BF)


def join_top(mine, mirror, ends, mirror_ends, inverse, sent, out, *, level):
    width = inverse.shape[1]
    gram_mine, gram_mirror = ends[:width], mirror_ends[:width]
    own, other = mine[:width], mine[width:]
    mirror_own, mirror_other = mirror[:width], mirror[width:]
    first = times(gram_mine, own).astype(BF)
    second = times(gram_mirror, other).astype(BF)
    matrix = inverse[level]
    out[:width] = (gram(matrix, matrix) + gram(own, first) + gram(other, second)).astype(BF)
    out[width : 2 * width] = (gram(mirror_other, first) + gram(mirror_own, second)).astype(BF)
    right, mirror_right = top_rights(ends, mirror_ends)
    cols = right.shape[0]
    out[2 * width : 2 * width + cols] = (-times(right, first) - times(mirror_right, second)).astype(BF)
    out[2 * width + cols :] = sent[...]


def top_rights(mine, mirror):
    width = mine.shape[1]
    cols = (mine.shape[0] - width) // 2
    right = mine[width : width + cols].astype(F32) - mirror[width + cols :].astype(F32)
    mirror_right = mirror[width : width + cols].astype(F32) - mine[width + cols :].astype(F32)
    return right.astype(BF), mirror_right.astype(BF)


def join_own(joined, joined_mate, solved, product, part, delta, folded, base, *, home):
    rows, width = part.shape[1], joined.shape[1]
    mine, mate = joined[2 * width + rows :], joined_mate[2 * width + rows :]
    for at, (a, b, matrices) in enumerate(((mine, mate, joined), (mate, mine, joined_mate))):
        change = (a[rows:].astype(F32) - b[:rows].astype(F32)).astype(BF)
        delta[at] = change
        part[at] = times(change, matrices[:width]) + matrices[2 * width : 2 * width + rows].astype(F32)
    total = solved[...]
    for side, at in enumerate((0, 1) if home else (1, 0)):
        matrices = (joined, joined_mate)[at]
        total = total - times(part[at].astype(BF), product[side])
        folded[side] = times(matrices[width : 2 * width], product[side]).astype(BF)
    base[...] = total


def join(theirs, across, base, folded, delta, below, *, home):
    rows = base.shape[0]
    for at, (a, b) in enumerate(((theirs, across), (across, theirs))):
        delta[at] = (a[rows:].astype(F32) - b[:rows].astype(F32)).astype(BF)
    own, other = (delta[0], delta[1]) if home else (delta[1], delta[0])
    below[...] = (base[...] - times(own, folded[0]) - times(other, folded[1])).astype(BF)


def join_blocks(part, delta, joined, joined_mate, block, block_mate):
    width = joined.shape[1]
    block[...] = part[0] + times(delta[0], joined[width : 2 * width])
    value = part[1] + times(delta[1], joined_mate[width : 2 * width])
    block_mate[...] = value.astype(BF)


def top_blocks(mine, mirror, ends, mirror_ends, delta, delta_mirror, out, mirrored):
    width = out.shape[1]
    right, mirror_right = top_rights(ends, mirror_ends)
    change, other = delta[0], delta_mirror[0]
    own = right.astype(F32) - times_t(change, mine[:width])
    own = own - times_t(other, mirror[width:])
    theirs = mirror_right.astype(F32) - times_t(other, mirror[:width])
    theirs = theirs - times_t(change, mine[width:])
    out[...] = times(own.astype(BF), ends[:width])
    mirrored[...] = times(theirs.astype(BF), mirror_ends[:width]).astype(BF)


def solve(delta, inverse, solved, *, level):
    step = times_t(delta[...], inverse[level]).astype(BF)
    solved[...] = times(step, inverse[level])


def top(mine, received, product, solved, out, out_bf, delta):
    rows = solved.shape[0]
    own = (mine[rows:].astype(F32) - received[:rows].astype(F32)).astype(BF)
    other = (received[rows:].astype(F32) - mine[:rows].astype(F32)).astype(BF)
    value = solved[...] - times(own, product[0]) - times(other, product[1])
    out[...] = value
    out_bf[...] = value.astype(BF)
    delta[0] = own
    delta[1] = other


def top_values(delta, own, mirror, out, mirrored):
    out[...] = times(delta[0], own[...])
    mirrored[...] = times(delta[1], mirror[...]).astype(BF)


def back_part(solved, known, product, out, *, side):
    out[...] = solved[...] - times(known[...].astype(BF), product[side])


def back(part, received, product, *outs, side):
    value = part[...] - times(received[...].astype(BF), product[side])
    for out in outs:
        out[...] = value.astype(out.dtype)


def back_both(received, known, solved, product, *outs):
    value = solved[...] - times(known[...], product[0])
    value = value - times(received[...].astype(BF), product[1])
    for out in outs:
        out[...] = value.astype(out.dtype)


def leaf_part(leaf, inverse, leaf_products, *refs, early):
    *mirrored, out = refs
    total = times(leaf[...].astype(BF), inverse[...])
    for level, block in zip(early, mirrored, strict=True):
        total = total - times(block[...], leaf_products[level])
    out[...] = total


def finish(part, leaf_products, *refs, late):
    *refs, leaf, out = refs
    mirrored, blocks = refs[: len(late)], refs[len(late) :]
    total = part[...]
    for level, block in zip(late, mirrored, strict=True):
        total = total - times(block[...].astype(BF), leaf_products[level])
    leaf[...] = total
    for level, block in enumerate(blocks):
        out[level] = block[...].astype(F32)


def shards(leaf_values, leaf_inverse, leaf_coupling, block_values, block_inverse, block_coupling):
    levels, width = block_inverse.shape[1], block_inverse.shape[2]
    size, cols = leaf_values.shape
    core = lax.axis_size("gy").bit_length() - 1
    inverse, coupling = block_inverse[0], block_coupling[0, :, 0]
    leaf_inv, leaf_cpl = leaf_inverse[0], leaf_coupling[0]
    values = jnp.swapaxes(block_values[0], 1, 2)
    vec, vec_bf, pair = ((cols, width), F32), ((cols, width), BF), ((2, width, width), BF)
    slab = ((1, cols, width), F32)

    def send(value, level, cross=False):
        return exchange(value, level, core, cross)

    def mate(value):
        return exchange(value, core, core)

    def arrived(value):
        return value.astype(F32)

    def after(value, other):
        return lax.optimization_barrier((value, other))[0]

    below_top = levels - 1
    first_across = 1 + (core - 1) % 2
    at_home = [
        level < first_across or level >= core or (level - first_across) % 2 == 1
        for level in range(levels)
    ]
    leaf = times_t(leaf_values.T.astype(BF), leaf_inv)
    terms = jnp.einsum("kwn,rn->krw", leaf_cpl, leaf.astype(BF), preferred_element_type=F32)
    received = send(terms[0].astype(BF), 0)
    product, ahead, solved = [None] * below_top, [None] * below_top, [None] * below_top
    joined = levels == core + 2 and core >= 3 and core % 2 == 1
    own_gram = call(top_gram, [((width, width), BF)], inverse)
    inverse_later = after(inverse, own_gram)
    if joined:
        pack, ahead[1], lowest = call(
            early_products, [((2 * width, width), BF), ((width + cols, width), BF), pair],
            inverse_later, coupling, terms, level=core,
        )
        mirror_pack = send(pack, below_top)
        inverse_later = after(inverse, pack)
        ends = call(top_ends, [((width + 2 * cols, width), BF)], own_gram, terms, values, cost=0)
    for level in range(core - 2 if joined else below_top):
        product[level] = call(
            products, [pair], inverse_later, coupling, level=level, cost=8 if level == 0 else 1
        )
    for level in range(core):
        if not at_home[level] and ahead[level] is None:
            ahead[level] = call(
                products_ahead, [((width + cols, width), BF)], inverse_later, coupling, terms, level=level
            )

    residue, change = values, None
    for level in range(core if joined else below_top):
        below = change
        if joined and level == core - 1:
            below, mirror_pack = lax.optimization_barrier((below, mirror_pack))
            change, out = call(
                forward_last, [vec_bf, ((2 * cols, width), BF)], arrived(received), below,
                below_turned, last_turned, terms, values, level=level, cost=4,
            )
            received = send(out, below_top, True)
        elif level == levels - 2:
            received, mirror_gram = lax.optimization_barrier((received, mirror_gram))
            change, out = call(
                forward_top, [vec_bf, ((2 * cols, width), BF)],
                residue, received, product[level], terms, values, level=level,
            )
            received = send(out, below_top)
        else:
            across = first_across <= level + 1 < core
            if not at_home[level]:
                if joined and level == core - 2:
                    ahead[level], ends = lax.optimization_barrier((ahead[level], ends))
                change, out = call(
                    forward_mate, [vec_bf, vec_bf], arrived(received), residue, ahead[level], cost=2
                )
            elif level and not at_home[level - 1]:
                change, out = call(
                    forward_back, [vec_bf, vec_bf], arrived(received), below,
                    product[level - 1], product[level], terms, values, level=level, cost=1,
                )
            elif joined and level == 0:
                change, out, residue = call(
                    forward_lowest, [vec_bf, vec_bf, vec_bf],
                    residue, received, lowest, terms, values, cost=0,
                )
            elif not at_home[level + 1]:
                change, out, residue = call(
                    forward_ahead, [vec_bf, vec_bf, vec_bf],
                    residue, received, product[level], terms, values, level=level,
                )
            else:
                change, out = call(
                    forward, [vec_bf, vec_bf], residue, received, product[level], terms, level=level
                )
            received = send(out, level + 1, across)
            if joined and level == core - 2:
                product[core - 1], last_turned, product[core - 2], below_turned = call(
                    products_last, [pair, pair, pair, ((width, width), BF)],
                    after(inverse, out), coupling, level=core - 1, cost=1,
                )
            if level == 0:
                if joined:
                    mirror_ends = send(after(ends, out), below_top)
                else:
                    mirror_gram = send(after(own_gram, out), below_top)
            if not at_home[level]:
                change = mate(change)
            elif not at_home[level + 1]:
                residue = mate(residue)
                ahead[level + 1] = mate(after(ahead[level + 1], out))
            else:
                residue = call(
                    forward_residue, [slab], change, product[level], values, level=level, cost=0
                )
        solved[level] = call(solve, [vec], change, inverse, level=level, cost=8 if level == core - 1 else 1)
    leaf_prod = jnp.einsum("kwn,nm->kwm", leaf_cpl, leaf_inv, preferred_element_type=F32).astype(BF)

    mates = [level for level in range(core) if level % 2 == 0]
    for level in mates:
        product[level] = mate(after(product[level], out))
        solved[level] = mate(after(solved[level], out))
    blocks, mirrored = [None] * levels, [None] * levels
    if joined:
        mirror_ends = after(mirror_ends, out)
        matrices = call(
            join_top, [((2 * width + 3 * cols, width), BF)],
            pack, mirror_pack, ends, mirror_ends, inverse, out, level=core, cost=1,
        )
        matrices_mate = mate(matrices)
        both, both_bf = ((2, cols, width), F32), ((2, cols, width), BF)
        at_own = core - 1 not in mates
        part, delta, folded, base = call(
            join_own, [both, both_bf, pair, vec],
            matrices, matrices_mate, solved[core - 1], product[core - 1], home=at_own,
        )
        theirs = mate(received)
        delta_mirror, block_bf = call(
            join, [both_bf, vec_bf], theirs, received, base, folded, home=at_own
        )
        blocks[core], mirrored[core] = call(
            join_blocks, [vec, vec_bf], part, delta_mirror, matrices, matrices_mate
        )
        blocks[-1], mirrored[-1] = call(
            top_blocks, [vec, vec_bf], pack, mirror_pack, ends, mirror_ends, delta, delta_mirror
        )
        if core - 1 not in mates:
            blocks[core - 1] = block_bf
        solved_above = core - 1
    else:
        top_pair = call(top_products, [pair], own_gram, mirror_gram, product[-1], cost=8)
        block, block_bf, deltas = call(
            top, [vec, vec_bf, ((2, cols, width), BF)], out, received, top_pair, solved[-1]
        )
        blocks[levels - 2] = block
        received = mirrored[levels - 2] = send(block_bf, levels - 2)
        blocks[-1], mirrored[-1] = call(top_values, [vec, vec_bf], deltas, own_gram, mirror_gram)
        solved_above = levels - 2
    late = [0]
    def pass_on(level, home):
        received = send(block_bf, level, level < core)
        if home == (level < core):
            mirrored[level] = mate(received)
            late.append(level)
        else:
            mirrored[level] = received
        return received

    if joined:
        received = pass_on(solved_above, solved_above not in mates)
    for level in reversed(range(solved_above)):
        home = level not in mates
        outs = [vec, vec_bf] if home else [vec_bf]
        if level + 1 >= core:
            side = 0 if home else 1
            part = call(back_part, [vec], solved[level], block_bf, product[level], side=side)
            made = call(back, outs, part, received, product[level], side=1 - side)
        else:
            known = mate(block_bf)
            if home:
                blocks[level + 1] = known
            made = call(back_both, outs, arrived(received), known, solved[level], product[level])
        if home:
            blocks[level], block_bf = made
        else:
            block_bf = made
        received = pass_on(level, home)
    if 0 in mates:
        blocks[0] = mate(block_bf)
    early = tuple(level for level in range(levels) if level not in late)
    part = call(
        leaf_part, [((cols, size), F32)],
        leaf, leaf_inv, leaf_prod, *[mirrored[level] for level in early], early=early,
    )
    mirrored[0] = arrived(mirrored[0])
    leaf_solution, stacked = call(
        finish, [((cols, size), F32), ((levels, cols, width), F32)],
        part, leaf_prod, *[mirrored[level] for level in late], *blocks, late=tuple(late),
    )
    return leaf_solution.T, jnp.swapaxes(stacked, 1, 2)[None]


def solution(mesh):
    both = ("gx", "gy")
    return jax.shard_map(
        shards,
        mesh=mesh,
        in_specs=tuple(P(both, *[None] * rank) for rank in (1, 2, 3, 3, 3, 5)),
        out_specs=(P(both, None), P(both, None, None, None)),
        check_vma=False,
    )
```

```python
import functools

import jax
import jax.numpy as jnp
from jax import lax
from jax.experimental import pallas as pl
from jax.experimental.pallas import tpu as pltpu
from jax.sharding import PartitionSpec as P

BF = jnp.bfloat16
F32 = jnp.float32
VMEM = pl.BlockSpec(memory_space=pltpu.VMEM)


def times(values, matrix):
    return lax.dot_general(values, matrix, (((1,), (0,)), ((), ())), preferred_element_type=F32)


def times_t(values, matrix):
    return lax.dot_general(values, matrix, (((1,), (1,)), ((), ())), preferred_element_type=F32)


def gram(left, right):
    return lax.dot_general(left, right, (((0,), (0,)), ((), ())), preferred_element_type=F32)


def turned(inverse, coupling):
    return lax.dot_general(inverse, coupling, (((0,), (1,)), ((), ())), preferred_element_type=F32)


def exchange(value, level, gy_levels, cross=False):
    inner, outer = lax.axis_size("gy"), lax.axis_size("gx")
    mask = 2**level ^ (inner if cross else 0)
    pairs = [(source, source ^ mask) for source in range(inner * outer)]
    return lax.ppermute(value, ("gx", "gy"), pairs)


def call(body, outs, *args, cost=1, **static):
    moved = sum(a.size * a.dtype.itemsize for a in args)
    made = pl.pallas_call(
        functools.partial(body, **static),
        out_shape=[jax.ShapeDtypeStruct(shape, kind) for shape, kind in outs],
        in_specs=[VMEM] * len(args),
        out_specs=[VMEM] * len(outs),
        compiler_params=pltpu.CompilerParams(vmem_limit_bytes=32 * 2**20),
        cost_estimate=pl.CostEstimate(flops=cost * 3 * 10**8, bytes_accessed=moved, transcendentals=0),
    )(*args)
    return made if len(outs) > 1 else made[0]


def products(inverse, coupling, out, *, level):
    for side in range(2):
        out[side] = times(coupling[level, side], inverse[level]).astype(BF)


def products_ahead(inverse, coupling, terms, ahead, *, level):
    rows = inverse.shape[1]
    ahead[:rows] = turned(inverse[level], coupling[level, 1]).astype(BF)
    ahead[rows:] = terms[level + 1].astype(BF)


def products_last(inverse, coupling, terms, values, out, out_turned, below, below_turned, folded, fixed, *, level):
    for side in range(2):
        out[side] = times(coupling[level, side], inverse[level]).astype(BF)
        below[side] = times(coupling[level - 1, side], inverse[level - 1]).astype(BF)
        out_turned[side] = turned(inverse[level], coupling[level, side]).astype(BF)
    below_turned[...] = turned(inverse[level - 1], coupling[level - 1, 0]).astype(BF)
    for side in range(2):
        folded[side] = times(below_turned[...], out_turned[side]).astype(BF)
    right = values[level].astype(BF)
    fixed[0] = values[level + 1] - times(right, out_turned[0])
    fixed[1] = terms[level + 1] + times(right, out_turned[1])


def top_gram(inverse, out):
    matrix = inverse[inverse.shape[0] - 1]
    out[...] = gram(matrix, matrix).astype(BF)


def top_products(own, mirror, product, out):
    out[0] = times(own[...], product[0]).astype(BF)
    out[1] = times(mirror[...], product[1]).astype(BF)


def forward(residue, received, product, terms, delta, out, *, level):
    change = (residue[0] - received[...].astype(F32)).astype(BF)
    delta[...] = change
    out[...] = (terms[level + 1] + times_t(change, product[1])).astype(BF)


def forward_ahead(residue, received, product, terms, values, delta, out, ahead, *, level):
    change = (residue[0] - received[...].astype(F32)).astype(BF)
    delta[...] = change
    out[...] = (terms[level + 1] + times_t(change, product[1])).astype(BF)
    ahead[...] = (values[level + 1] - times_t(change, product[0])).astype(BF)


def forward_mate(received, residue, ahead, delta, out):
    rows = ahead.shape[1]
    change = (residue[...].astype(F32) - received[...].astype(F32)).astype(BF)
    delta[...] = change
    out[...] = (ahead[rows:].astype(F32) + times(change, ahead[:rows])).astype(BF)


def forward_back(received, below, product_below, product, terms, values, delta, out, *, level):
    residue = values[level] - times_t(below[...], product_below[0])
    change = (residue - received[...].astype(F32)).astype(BF)
    delta[...] = change
    out[...] = (terms[level + 1] + times_t(change, product[1])).astype(BF)


def forward_residue(delta, product, values, residue, *, level):
    residue[0] = values[level + 1] - times_t(delta[...], product[0])


def forward_top(residue, received, product, terms, values, delta, out, *, level):
    change = (residue[0] - received[...].astype(F32)).astype(BF)
    delta[...] = change
    rows = change.shape[0]
    out[:rows] = (terms[level + 1] + times_t(change, product[1])).astype(BF)
    out[rows:] = (values[level + 1] - times_t(change, product[0])).astype(BF)


def forward_lowest(residue, received, product, terms, values, delta, out, ahead):
    change = (residue[0] - received[...].astype(F32)).astype(BF)
    delta[...] = change
    out[...] = (terms[1] + times(change, product[1])).astype(BF)
    ahead[...] = (values[1] - times(change, product[0])).astype(BF)


def forward_last(received, below, folded, product, fixed, out):
    rows, arrived = received.shape[0], received[...].astype(BF)
    out[:rows] = (fixed[1] - times(below[...], folded[1]) - times(arrived, product[1])).astype(BF)
    out[rows:] = (fixed[0] + times(below[...], folded[0]) + times(arrived, product[0])).astype(BF)


def solve_last(received, below, below_turned, inverse, values, solved, *, level):
    residue = values[level] - times(below[...], below_turned[...])
    change = (residue - received[...].astype(F32)).astype(BF)
    step = times_t(change, inverse[level]).astype(BF)
    solved[...] = times(step, inverse[level])


def early_products(inverse, coupling, terms, pack, ahead, lowest, *, level):
    width = inverse.shape[1]
    for side in range(2):
        made = times(coupling[level, side], inverse[level]).astype(BF)
        pack[side * width : (side + 1) * width] = made
        lowest[side] = turned(inverse[0], coupling[0, side]).astype(BF)
    products_ahead(inverse, coupling, terms, ahead, level=1)


def top_ends(own_gram, terms, values, out):
    width, cols = own_gram.shape[0], values.shape[1]
    out[:width] = own_gram[...]
    out[width : width + cols] = values[values.shape[0] - 1].astype(BF)
    out[width + cols :] = terms[terms.shape[0] - 1].astype(BF)


def join_top(mine, mirror, ends, mirror_ends, inverse, sent, out, *, level):
    width = inverse.shape[1]
    gram_mine, gram_mirror = ends[:width], mirror_ends[:width]
    own, other = mine[:width], mine[width:]
    mirror_own, mirror_other = mirror[:width], mirror[width:]
    first = times(gram_mine, own).astype(BF)
    second = times(gram_mirror, other).astype(BF)
    matrix = inverse[level]
    out[:width] = (gram(matrix, matrix) + gram(own, first) + gram(other, second)).astype(BF)
    out[width : 2 * width] = (gram(mirror_other, first) + gram(mirror_own, second)).astype(BF)
    right, mirror_right = top_rights(ends, mirror_ends)
    cols = right.shape[0]
    out[2 * width : 2 * width + cols] = (-times(right, first) - times(mirror_right, second)).astype(BF)
    out[2 * width + cols :] = sent[...]


def top_rights(mine, mirror):
    width = mine.shape[1]
    cols = (mine.shape[0] - width) // 2
    right = mine[width : width + cols].astype(F32) - mirror[width + cols :].astype(F32)
    mirror_right = mirror[width : width + cols].astype(F32) - mine[width + cols :].astype(F32)
    return right.astype(BF), mirror_right.astype(BF)


def join_own(joined, joined_mate, solved, product, part, delta, folded, base, *, home):
    rows, width = part.shape[1], joined.shape[1]
    mine, mate = joined[2 * width + rows :], joined_mate[2 * width + rows :]
    for at, (a, b, matrices) in enumerate(((mine, mate, joined), (mate, mine, joined_mate))):
        change = (a[rows:].astype(F32) - b[:rows].astype(F32)).astype(BF)
        delta[at] = change
        part[at] = times(change, matrices[:width]) + matrices[2 * width : 2 * width + rows].astype(F32)
    total = solved[...]
    for side, at in enumerate((0, 1) if home else (1, 0)):
        matrices = (joined, joined_mate)[at]
        total = total - times(part[at].astype(BF), product[side])
        folded[side] = times(matrices[width : 2 * width], product[side]).astype(BF)
    base[...] = total


def join(theirs, across, base, folded, delta, below, *, home):
    rows = base.shape[0]
    for at, (a, b) in enumerate(((theirs, across), (across, theirs))):
        delta[at] = (a[rows:].astype(F32) - b[:rows].astype(F32)).astype(BF)
    own, other = (delta[0], delta[1]) if home else (delta[1], delta[0])
    below[...] = (base[...] - times(own, folded[0]) - times(other, folded[1])).astype(BF)


def join_blocks(part, delta, joined, joined_mate, block, block_mate):
    width = joined.shape[1]
    block[...] = part[0] + times(delta[0], joined[width : 2 * width])
    value = part[1] + times(delta[1], joined_mate[width : 2 * width])
    block_mate[...] = value.astype(BF)


def top_blocks(mine, mirror, ends, mirror_ends, delta, delta_mirror, out, mirrored):
    width = out.shape[1]
    right, mirror_right = top_rights(ends, mirror_ends)
    change, other = delta[0], delta_mirror[0]
    own = right.astype(F32) - times_t(change, mine[:width])
    own = own - times_t(other, mirror[width:])
    theirs = mirror_right.astype(F32) - times_t(other, mirror[:width])
    theirs = theirs - times_t(change, mine[width:])
    out[...] = times(own.astype(BF), ends[:width])
    mirrored[...] = times(theirs.astype(BF), mirror_ends[:width]).astype(BF)


def solve(delta, inverse, solved, *, level):
    step = times_t(delta[...], inverse[level]).astype(BF)
    solved[...] = times(step, inverse[level])


def top(mine, received, product, solved, out, out_bf, delta):
    rows = solved.shape[0]
    own = (mine[rows:].astype(F32) - received[:rows].astype(F32)).astype(BF)
    other = (received[rows:].astype(F32) - mine[:rows].astype(F32)).astype(BF)
    value = solved[...] - times(own, product[0]) - times(other, product[1])
    out[...] = value
    out_bf[...] = value.astype(BF)
    delta[0] = own
    delta[1] = other


def top_values(delta, own, mirror, out, mirrored):
    out[...] = times(delta[0], own[...])
    mirrored[...] = times(delta[1], mirror[...]).astype(BF)


def back_part(solved, known, product, out, *, side):
    out[...] = solved[...] - times(known[...].astype(BF), product[side])


def back(part, received, product, *outs, side):
    value = part[...] - times(received[...].astype(BF), product[side])
    for out in outs:
        out[...] = value.astype(out.dtype)


def back_both(received, known, solved, product, *outs):
    value = solved[...] - times(known[...], product[0])
    value = value - times(received[...].astype(BF), product[1])
    for out in outs:
        out[...] = value.astype(out.dtype)


def leaf_part(leaf, inverse, leaf_products, *refs, early):
    *mirrored, out = refs
    total = times(leaf[...].astype(BF), inverse[...])
    for level, block in zip(early, mirrored, strict=True):
        total = total - times(block[...], leaf_products[level])
    out[...] = total


def finish(part, leaf_products, *refs, late):
    *refs, leaf, out = refs
    mirrored, blocks = refs[: len(late)], refs[len(late) :]
    total = part[...]
    for level, block in zip(late, mirrored, strict=True):
        total = total - times(block[...].astype(BF), leaf_products[level])
    leaf[...] = total
    for level, block in enumerate(blocks):
        out[level] = block[...].astype(F32)


def shards(leaf_values, leaf_inverse, leaf_coupling, block_values, block_inverse, block_coupling):
    levels, width = block_inverse.shape[1], block_inverse.shape[2]
    size, cols = leaf_values.shape
    core = lax.axis_size("gy").bit_length() - 1
    inverse, coupling = block_inverse[0], block_coupling[0, :, 0]
    leaf_inv, leaf_cpl = leaf_inverse[0], leaf_coupling[0]
    values = jnp.swapaxes(block_values[0], 1, 2)
    vec, vec_bf, pair = ((cols, width), F32), ((cols, width), BF), ((2, width, width), BF)
    slab = ((1, cols, width), F32)

    def send(value, level, cross=False):
        return exchange(value, level, core, cross)

    def mate(value):
        return exchange(value, core, core)

    def arrived(value):
        return value.astype(F32)

    def after(value, other):
        return lax.optimization_barrier((value, other))[0]

    below_top = levels - 1
    first_across = 1 + (core - 1) % 2
    at_home = [
        level < first_across or level >= core or (level - first_across) % 2 == 1
        for level in range(levels)
    ]
    leaf = times_t(leaf_values.T.astype(BF), leaf_inv)
    terms = jnp.einsum("kwn,rn->krw", leaf_cpl, leaf.astype(BF), preferred_element_type=F32)
    received = send(terms[0].astype(BF), 0)
    product, ahead, solved = [None] * below_top, [None] * below_top, [None] * below_top
    joined = levels == core + 2 and core >= 3 and core % 2 == 1
    own_gram = call(top_gram, [((width, width), BF)], inverse)
    inverse_later = after(inverse, own_gram)
    if joined:
        pack, ahead[1], lowest = call(
            early_products, [((2 * width, width), BF), ((width + cols, width), BF), pair],
            inverse_later, coupling, terms, level=core,
        )
        mirror_pack = send(pack, below_top)
        inverse_later = after(inverse, pack)
        ends = call(top_ends, [((width + 2 * cols, width), BF)], own_gram, terms, values, cost=0)
    for level in range(core - 2 if joined else below_top):
        product[level] = call(
            products, [pair], inverse_later, coupling, level=level, cost=8 if level == 0 else 1
        )
    for level in range(core):
        if not at_home[level] and ahead[level] is None:
            ahead[level] = call(
                products_ahead, [((width + cols, width), BF)], inverse_later, coupling, terms, level=level
            )

    residue, change = values, None
    for level in range(core if joined else below_top):
        below = change
        if joined and level == core - 1:
            below, mirror_pack = lax.optimization_barrier((below, mirror_pack))
            last = arrived(received)
            out = call(
                forward_last, [((2 * cols, width), BF)],
                last, below, folded, last_turned, fixed, cost=4,
            )
            received = send(out, below_top, True)
        elif level == levels - 2:
            received, mirror_gram = lax.optimization_barrier((received, mirror_gram))
            change, out = call(
                forward_top, [vec_bf, ((2 * cols, width), BF)],
                residue, received, product[level], terms, values, level=level,
            )
            received = send(out, below_top)
        else:
            across = first_across <= level + 1 < core
            if not at_home[level]:
                if joined and level == core - 2:
                    ahead[level], ends = lax.optimization_barrier((ahead[level], ends))
                change, out = call(
                    forward_mate, [vec_bf, vec_bf], received, residue, ahead[level], cost=2
                )
            elif level and not at_home[level - 1]:
                change, out = call(
                    forward_back, [vec_bf, vec_bf], arrived(received), below,
                    product[level - 1], product[level], terms, values, level=level, cost=1,
                )
            elif joined and level == 0:
                change, out, residue = call(
                    forward_lowest, [vec_bf, vec_bf, vec_bf],
                    residue, received, lowest, terms, values, cost=0,
                )
            elif not at_home[level + 1]:
                change, out, residue = call(
                    forward_ahead, [vec_bf, vec_bf, vec_bf],
                    residue, received, product[level], terms, values, level=level,
                )
            else:
                change, out = call(
                    forward, [vec_bf, vec_bf], residue, received, product[level], terms, level=level
                )
            received = send(out, level + 1, across)
            if joined and level == core - 2:
                product[core - 1], last_turned, product[core - 2], below_turned, folded, fixed = call(
                    products_last,
                    [pair, pair, pair, ((width, width), BF), pair, ((2, cols, width), F32)],
                    after(inverse, out), coupling, terms, values, level=core - 1, cost=1,
                )
            if level == 0:
                if joined:
                    mirror_ends = send(after(ends, out), below_top)
                else:
                    mirror_gram = send(after(own_gram, out), below_top)
            if not at_home[level]:
                change = mate(change)
            elif not at_home[level + 1]:
                residue = mate(residue)
                ahead[level + 1] = mate(after(ahead[level + 1], out))
            else:
                residue = call(
                    forward_residue, [slab], change, product[level], values, level=level, cost=0
                )
        if joined and level == core - 1:
            solved[level] = call(
                solve_last, [vec], last, below, below_turned, inverse, values, level=level, cost=8
            )
        else:
            solved[level] = call(solve, [vec], change, inverse, level=level)
    leaf_prod = jnp.einsum("kwn,nm->kwm", leaf_cpl, leaf_inv, preferred_element_type=F32).astype(BF)

    mates = [level for level in range(core) if level % 2 == 0]
    for level in mates:
        product[level] = mate(after(product[level], out))
        solved[level] = mate(after(solved[level], out))
    blocks, mirrored = [None] * levels, [None] * levels
    if joined:
        mirror_ends = after(mirror_ends, out)
        matrices = call(
            join_top, [((2 * width + 3 * cols, width), BF)],
            pack, mirror_pack, ends, mirror_ends, inverse, out, level=core, cost=1,
        )
        matrices_mate = mate(matrices)
        both, both_bf = ((2, cols, width), F32), ((2, cols, width), BF)
        at_own = core - 1 not in mates
        part, delta, folded, base = call(
            join_own, [both, both_bf, pair, vec],
            matrices, matrices_mate, solved[core - 1], product[core - 1], home=at_own,
        )
        theirs = mate(received)
        delta_mirror, block_bf = call(
            join, [both_bf, vec_bf], theirs, received, base, folded, home=at_own
        )
        blocks[core], mirrored[core] = call(
            join_blocks, [vec, vec_bf], part, delta_mirror, matrices, matrices_mate
        )
        blocks[-1], mirrored[-1] = call(
            top_blocks, [vec, vec_bf], pack, mirror_pack, ends, mirror_ends, delta, delta_mirror
        )
        if core - 1 not in mates:
            blocks[core - 1] = block_bf
        solved_above = core - 1
    else:
        top_pair = call(top_products, [pair], own_gram, mirror_gram, product[-1], cost=8)
        block, block_bf, deltas = call(
            top, [vec, vec_bf, ((2, cols, width), BF)], out, received, top_pair, solved[-1]
        )
        blocks[levels - 2] = block
        received = mirrored[levels - 2] = send(block_bf, levels - 2)
        blocks[-1], mirrored[-1] = call(top_values, [vec, vec_bf], deltas, own_gram, mirror_gram)
        solved_above = levels - 2
    late = [0]
    def pass_on(level, home):
        received = send(block_bf, level, level < core)
        if home == (level < core):
            mirrored[level] = mate(received)
            late.append(level)
        else:
            mirrored[level] = received
        return received

    if joined:
        received = pass_on(solved_above, solved_above not in mates)
    for level in reversed(range(solved_above)):
        home = level not in mates
        outs = [vec, vec_bf] if home else [vec_bf]
        if level + 1 >= core:
            side = 0 if home else 1
            part = call(back_part, [vec], solved[level], block_bf, product[level], side=side)
            made = call(back, outs, part, received, product[level], side=1 - side)
        else:
            known = mate(block_bf)
            if home:
                blocks[level + 1] = known
            made = call(back_both, outs, received, known, solved[level], product[level])
        if home:
            blocks[level], block_bf = made
        else:
            block_bf = made
        received = pass_on(level, home)
    if 0 in mates:
        blocks[0] = mate(block_bf)
    early = tuple(level for level in range(levels) if level not in late)
    part = call(
        leaf_part, [((cols, size), F32)],
        leaf, leaf_inv, leaf_prod, *[mirrored[level] for level in early], early=early,
    )
    leaf_solution, stacked = call(
        finish, [((cols, size), F32), ((levels, cols, width), F32)],
        part, leaf_prod, *[mirrored[level] for level in late], *blocks, late=tuple(late),
    )
    return leaf_solution.T, jnp.swapaxes(stacked, 1, 2)[None]


def solution(mesh):
    both = ("gx", "gy")
    return jax.shard_map(
        shards,
        mesh=mesh,
        in_specs=tuple(P(both, *[None] * rank) for rank in (1, 2, 3, 3, 3, 5)),
        out_specs=(P(both, None), P(both, None, None, None)),
        check_vma=False,
    )
```

```python
import functools

import jax
import jax.numpy as jnp
from jax import lax
from jax.experimental import pallas as pl
from jax.experimental.pallas import tpu as pltpu
from jax.sharding import PartitionSpec as P

BF = jnp.bfloat16
F32 = jnp.float32
VMEM = pl.BlockSpec(memory_space=pltpu.VMEM)


def times(values, matrix):
    return lax.dot_general(values, matrix, (((1,), (0,)), ((), ())), preferred_element_type=F32)


def times_t(values, matrix):
    return lax.dot_general(values, matrix, (((1,), (1,)), ((), ())), preferred_element_type=F32)


def gram(left, right):
    return lax.dot_general(left, right, (((0,), (0,)), ((), ())), preferred_element_type=F32)


def turned(inverse, coupling):
    return lax.dot_general(inverse, coupling, (((0,), (1,)), ((), ())), preferred_element_type=F32)


def exchange(value, level, gy_levels, cross=False):
    inner, outer = lax.axis_size("gy"), lax.axis_size("gx")
    mask = 2**level ^ (inner if cross else 0)
    pairs = [(source, source ^ mask) for source in range(inner * outer)]
    return lax.ppermute(value, ("gx", "gy"), pairs)


def call(body, outs, *args, cost=1, **static):
    moved = sum(a.size * a.dtype.itemsize for a in args)
    made = pl.pallas_call(
        functools.partial(body, **static),
        out_shape=[jax.ShapeDtypeStruct(shape, kind) for shape, kind in outs],
        in_specs=[VMEM] * len(args),
        out_specs=[VMEM] * len(outs),
        compiler_params=pltpu.CompilerParams(vmem_limit_bytes=32 * 2**20),
        cost_estimate=pl.CostEstimate(flops=cost * 3 * 10**8, bytes_accessed=moved, transcendentals=0),
    )(*args)
    return made if len(outs) > 1 else made[0]


def products(inverse, coupling, out, *, level):
    for side in range(2):
        out[side] = times(coupling[level, side], inverse[level]).astype(BF)


def products_ahead(inverse, coupling, terms, ahead, *, level):
    rows = inverse.shape[1]
    ahead[:rows] = turned(inverse[level], coupling[level, 1]).astype(BF)
    ahead[rows:] = terms[level + 1].astype(BF)


def products_last(inverse, coupling, terms, values, out, out_turned, below, below_turned, folded, fixed, *, level):
    for side in range(2):
        out[side] = times(coupling[level, side], inverse[level]).astype(BF)
        below[side] = times(coupling[level - 1, side], inverse[level - 1]).astype(BF)
        out_turned[side] = turned(inverse[level], coupling[level, side]).astype(BF)
    below_turned[...] = turned(inverse[level - 1], coupling[level - 1, 0]).astype(BF)
    for side in range(2):
        folded[side] = times(below_turned[...], out_turned[side]).astype(BF)
    right = values[level].astype(BF)
    fixed[0] = values[level + 1] - times(right, out_turned[0])
    fixed[1] = terms[level + 1] + times(right, out_turned[1])


def top_gram(inverse, out):
    matrix = inverse[inverse.shape[0] - 1]
    out[...] = gram(matrix, matrix).astype(BF)


def top_products(own, mirror, product, out):
    out[0] = times(own[...], product[0]).astype(BF)
    out[1] = times(mirror[...], product[1]).astype(BF)


def forward(residue, received, product, terms, delta, out, *, level):
    change = (residue[0] - received[...].astype(F32)).astype(BF)
    delta[...] = change
    out[...] = (terms[level + 1] + times_t(change, product[1])).astype(BF)


def forward_ahead(residue, received, product, terms, values, delta, out, ahead, *, level):
    change = (residue[0] - received[...].astype(F32)).astype(BF)
    delta[...] = change
    out[...] = (terms[level + 1] + times_t(change, product[1])).astype(BF)
    ahead[...] = (values[level + 1] - times_t(change, product[0])).astype(BF)


def forward_mate(received, residue, ahead, delta, out):
    rows = ahead.shape[1]
    change = (residue[...].astype(F32) - received[...].astype(F32)).astype(BF)
    delta[...] = change
    out[...] = (ahead[rows:].astype(F32) + times(change, ahead[:rows])).astype(BF)


def forward_back(received, below, product_below, product, terms, values, delta, out, *ahead, level):
    residue = values[level] - times_t(below[...], product_below[0])
    change = (residue - received[...].astype(F32)).astype(BF)
    delta[...] = change
    out[...] = (terms[level + 1] + times_t(change, product[1])).astype(BF)
    for above in ahead:
        above[...] = (values[level + 1] - times_t(change, product[0])).astype(BF)


def forward_residue(delta, product, values, residue, *, level):
    residue[0] = values[level + 1] - times_t(delta[...], product[0])


def forward_top(residue, received, product, terms, values, delta, out, *, level):
    change = (residue[0] - received[...].astype(F32)).astype(BF)
    delta[...] = change
    rows = change.shape[0]
    out[:rows] = (terms[level + 1] + times_t(change, product[1])).astype(BF)
    out[rows:] = (values[level + 1] - times_t(change, product[0])).astype(BF)


def forward_lowest(residue, received, product, terms, values, delta, out, ahead):
    change = (residue[0] - received[...].astype(F32)).astype(BF)
    delta[...] = change
    out[...] = (terms[1] + times(change, product[1])).astype(BF)
    ahead[...] = (values[1] - times(change, product[0])).astype(BF)


def forward_last(received, below, folded, product, fixed, out):
    rows, arrived = received.shape[0], received[...].astype(BF)
    out[:rows] = (fixed[1] - times(below[...], folded[1]) - times(arrived, product[1])).astype(BF)
    out[rows:] = (fixed[0] + times(below[...], folded[0]) + times(arrived, product[0])).astype(BF)


def solve_last(received, below, below_turned, inverse, values, solved, *, level):
    residue = values[level] - times(below[...], below_turned[...])
    change = (residue - received[...].astype(F32)).astype(BF)
    step = times_t(change, inverse[level]).astype(BF)
    solved[...] = times(step, inverse[level])


def early_products(inverse, coupling, terms, pack, ahead, lowest, *, level):
    width = inverse.shape[1]
    for side in range(2):
        made = times(coupling[level, side], inverse[level]).astype(BF)
        pack[side * width : (side + 1) * width] = made
        lowest[side] = turned(inverse[0], coupling[0, side]).astype(BF)
    products_ahead(inverse, coupling, terms, ahead, level=1)


def top_ends(own_gram, terms, values, out):
    width, cols = own_gram.shape[0], values.shape[1]
    out[:width] = own_gram[...]
    out[width : width + cols] = values[values.shape[0] - 1].astype(BF)
    out[width + cols :] = terms[terms.shape[0] - 1].astype(BF)


def join_top(mine, mirror, ends, mirror_ends, inverse, sent, out, *, level):
    width = inverse.shape[1]
    gram_mine, gram_mirror = ends[:width], mirror_ends[:width]
    own, other = mine[:width], mine[width:]
    mirror_own, mirror_other = mirror[:width], mirror[width:]
    first = times(gram_mine, own).astype(BF)
    second = times(gram_mirror, other).astype(BF)
    matrix = inverse[level]
    out[:width] = (gram(matrix, matrix) + gram(own, first) + gram(other, second)).astype(BF)
    out[width : 2 * width] = (gram(mirror_other, first) + gram(mirror_own, second)).astype(BF)
    right, mirror_right = top_rights(ends, mirror_ends)
    cols = right.shape[0]
    out[2 * width : 2 * width + cols] = (-times(right, first) - times(mirror_right, second)).astype(BF)
    out[2 * width + cols :] = sent[...]


def top_rights(mine, mirror):
    width = mine.shape[1]
    cols = (mine.shape[0] - width) // 2
    right = mine[width : width + cols].astype(F32) - mirror[width + cols :].astype(F32)
    mirror_right = mirror[width : width + cols].astype(F32) - mine[width + cols :].astype(F32)
    return right.astype(BF), mirror_right.astype(BF)


def join_own(joined, joined_mate, solved, product, part, delta, folded, base, *, home):
    rows, width = part.shape[1], joined.shape[1]
    mine, mate = joined[2 * width + rows :], joined_mate[2 * width + rows :]
    for at, (a, b, matrices) in enumerate(((mine, mate, joined), (mate, mine, joined_mate))):
        change = (a[rows:].astype(F32) - b[:rows].astype(F32)).astype(BF)
        delta[at] = change
        part[at] = times(change, matrices[:width]) + matrices[2 * width : 2 * width + rows].astype(F32)
    total = solved[...]
    for side, at in enumerate((0, 1) if home else (1, 0)):
        matrices = (joined, joined_mate)[at]
        total = total - times(part[at].astype(BF), product[side])
        folded[side] = times(matrices[width : 2 * width], product[side]).astype(BF)
    base[...] = total


def join(theirs, across, base, folded, delta, below, *, home):
    rows = base.shape[0]
    for at, (a, b) in enumerate(((theirs, across), (across, theirs))):
        delta[at] = (a[rows:].astype(F32) - b[:rows].astype(F32)).astype(BF)
    own, other = (delta[0], delta[1]) if home else (delta[1], delta[0])
    below[...] = (base[...] - times(own, folded[0]) - times(other, folded[1])).astype(BF)


def join_blocks(part, delta, joined, joined_mate, block, block_mate):
    width = joined.shape[1]
    block[...] = part[0] + times(delta[0], joined[width : 2 * width])
    value = part[1] + times(delta[1], joined_mate[width : 2 * width])
    block_mate[...] = value.astype(BF)


def top_blocks(mine, mirror, ends, mirror_ends, delta, delta_mirror, out, mirrored):
    width = out.shape[1]
    right, mirror_right = top_rights(ends, mirror_ends)
    change, other = delta[0], delta_mirror[0]
    own = right.astype(F32) - times_t(change, mine[:width])
    own = own - times_t(other, mirror[width:])
    theirs = mirror_right.astype(F32) - times_t(other, mirror[:width])
    theirs = theirs - times_t(change, mine[width:])
    out[...] = times(own.astype(BF), ends[:width])
    mirrored[...] = times(theirs.astype(BF), mirror_ends[:width]).astype(BF)


def solve(delta, inverse, solved, *, level):
    step = times_t(delta[...], inverse[level]).astype(BF)
    solved[...] = times(step, inverse[level])


def top(mine, received, product, solved, out, out_bf, delta):
    rows = solved.shape[0]
    own = (mine[rows:].astype(F32) - received[:rows].astype(F32)).astype(BF)
    other = (received[rows:].astype(F32) - mine[:rows].astype(F32)).astype(BF)
    value = solved[...] - times(own, product[0]) - times(other, product[1])
    out[...] = value
    out_bf[...] = value.astype(BF)
    delta[0] = own
    delta[1] = other


def top_values(delta, own, mirror, out, mirrored):
    out[...] = times(delta[0], own[...])
    mirrored[...] = times(delta[1], mirror[...]).astype(BF)


def back_part(solved, known, product, out, *, side):
    out[...] = solved[...] - times(known[...].astype(BF), product[side])


def back(part, received, product, *outs, side):
    value = part[...] - times(received[...].astype(BF), product[side])
    for out in outs:
        out[...] = value.astype(out.dtype)


def back_both(received, known, solved, product, *outs):
    value = solved[...] - times(known[...], product[0])
    value = value - times(received[...].astype(BF), product[1])
    for out in outs:
        out[...] = value.astype(out.dtype)


def leaf_part(leaf, inverse, leaf_products, *refs, early):
    *mirrored, out = refs
    total = times(leaf[...].astype(BF), inverse[...])
    for level, block in zip(early, mirrored, strict=True):
        total = total - times(block[...], leaf_products[level])
    out[...] = total


def finish(part, leaf_products, *refs, late):
    *refs, leaf, out = refs
    mirrored, blocks = refs[: len(late)], refs[len(late) :]
    total = part[...]
    for level, block in zip(late, mirrored, strict=True):
        total = total - times(block[...].astype(BF), leaf_products[level])
    leaf[...] = total
    for level, block in enumerate(blocks):
        out[level] = block[...].astype(F32)


def shards(leaf_values, leaf_inverse, leaf_coupling, block_values, block_inverse, block_coupling):
    levels, width = block_inverse.shape[1], block_inverse.shape[2]
    size, cols = leaf_values.shape
    core = lax.axis_size("gy").bit_length() - 1
    inverse, coupling = block_inverse[0], block_coupling[0, :, 0]
    leaf_inv, leaf_cpl = leaf_inverse[0], leaf_coupling[0]
    values = jnp.swapaxes(block_values[0], 1, 2)
    vec, vec_bf, pair = ((cols, width), F32), ((cols, width), BF), ((2, width, width), BF)
    slab = ((1, cols, width), F32)

    def send(value, level, cross=False):
        return exchange(value, level, core, cross)

    def mate(value):
        return exchange(value, core, core)

    def arrived(value):
        return value.astype(F32)

    def after(value, other):
        return lax.optimization_barrier((value, other))[0]

    below_top = levels - 1
    first_across = 1 + (core - 1) % 2
    at_home = [
        level < first_across or level >= core or (level - first_across) % 2 == 1
        for level in range(levels)
    ]
    leaf = times_t(leaf_values.T.astype(BF), leaf_inv)
    terms = jnp.einsum("kwn,rn->krw", leaf_cpl, leaf.astype(BF), preferred_element_type=F32)
    received = send(terms[0].astype(BF), 0)
    product, ahead, solved = [None] * below_top, [None] * below_top, [None] * below_top
    joined = levels == core + 2 and core >= 3 and core % 2 == 1
    own_gram = call(top_gram, [((width, width), BF)], inverse)
    inverse_later = after(inverse, own_gram)
    if joined:
        pack, ahead[1], lowest = call(
            early_products, [((2 * width, width), BF), ((width + cols, width), BF), pair],
            inverse_later, coupling, terms, level=core,
        )
        mirror_pack = send(pack, below_top)
        inverse_later = after(inverse, pack)
        ends = call(top_ends, [((width + 2 * cols, width), BF)], own_gram, terms, values, cost=0)
    for level in range(core - 2 if joined else below_top):
        product[level] = call(
            products, [pair], inverse_later, coupling, level=level, cost=8 if level == 0 else 1
        )
    for level in range(core):
        if not at_home[level] and ahead[level] is None:
            ahead[level] = call(
                products_ahead, [((width + cols, width), BF)], inverse_later, coupling, terms, level=level
            )

    residue, change = values, None
    for level in range(core if joined else below_top):
        below = change
        if joined and level == core - 1:
            below, mirror_pack = lax.optimization_barrier((below, mirror_pack))
            last = arrived(received)
            out = call(
                forward_last, [((2 * cols, width), BF)],
                last, below, folded, last_turned, fixed, cost=4,
            )
            received = send(out, below_top, True)
        elif level == levels - 2:
            received, mirror_gram = lax.optimization_barrier((received, mirror_gram))
            change, out = call(
                forward_top, [vec_bf, ((2 * cols, width), BF)],
                residue, received, product[level], terms, values, level=level,
            )
            received = send(out, below_top)
        else:
            across = first_across <= level + 1 < core
            if not at_home[level]:
                if joined and level == core - 2:
                    ahead[level], ends = lax.optimization_barrier((ahead[level], ends))
                change, out = call(
                    forward_mate, [vec_bf, vec_bf], received, residue, ahead[level], cost=2
                )
            elif level and not at_home[level - 1]:
                change, out, *above = call(
                    forward_back, [vec_bf, vec_bf] + ([] if at_home[level + 1] else [vec_bf]),
                    arrived(received), below, product[level - 1], product[level], terms, values, level=level,
                )
                residue = above[0] if above else None
            elif joined and level == 0:
                change, out, residue = call(
                    forward_lowest, [vec_bf, vec_bf, vec_bf],
                    residue, received, lowest, terms, values, cost=0,
                )
            elif not at_home[level + 1]:
                change, out, residue = call(
                    forward_ahead, [vec_bf, vec_bf, vec_bf],
                    residue, received, product[level], terms, values, level=level,
                )
            else:
                change, out = call(
                    forward, [vec_bf, vec_bf], residue, received, product[level], terms, level=level
                )
            received = send(out, level + 1, across)
            if joined and level == core - 2:
                product[core - 1], last_turned, product[core - 2], below_turned, folded, fixed = call(
                    products_last,
                    [pair, pair, pair, ((width, width), BF), pair, ((2, cols, width), F32)],
                    after(inverse, out), coupling, terms, values, level=core - 1, cost=1,
                )
            if level == 0:
                if joined:
                    mirror_ends = send(after(ends, out), below_top)
                else:
                    mirror_gram = send(after(own_gram, out), below_top)
            if not at_home[level]:
                change = mate(change)
            elif not at_home[level + 1]:
                residue = mate(residue)
                ahead[level + 1] = mate(after(ahead[level + 1], out))
            else:
                residue = call(
                    forward_residue, [slab], change, product[level], values, level=level, cost=0
                )
        if joined and level == core - 1:
            solved[level] = call(
                solve_last, [vec], last, below, below_turned, inverse, values, level=level, cost=8
            )
        else:
            solved[level] = call(solve, [vec], change, inverse, level=level)
    leaf_prod = jnp.einsum("kwn,nm->kwm", leaf_cpl, leaf_inv, preferred_element_type=F32).astype(BF)

    mates = [level for level in range(core) if level % 2 == 0]
    for level in mates:
        product[level] = mate(after(product[level], out))
        solved[level] = mate(after(solved[level], out))
    blocks, mirrored = [None] * levels, [None] * levels
    if joined:
        mirror_ends = after(mirror_ends, out)
        matrices = call(
            join_top, [((2 * width + 3 * cols, width), BF)],
            pack, mirror_pack, ends, mirror_ends, inverse, out, level=core, cost=1,
        )
        matrices_mate = mate(matrices)
        both, both_bf = ((2, cols, width), F32), ((2, cols, width), BF)
        at_own = core - 1 not in mates
        part, delta, folded, base = call(
            join_own, [both, both_bf, pair, vec],
            matrices, matrices_mate, solved[core - 1], product[core - 1], home=at_own,
        )
        theirs = mate(received)
        delta_mirror, block_bf = call(
            join, [both_bf, vec_bf], theirs, received, base, folded, home=at_own
        )
        blocks[core], mirrored[core] = call(
            join_blocks, [vec, vec_bf], part, delta_mirror, matrices, matrices_mate
        )
        blocks[-1], mirrored[-1] = call(
            top_blocks, [vec, vec_bf], pack, mirror_pack, ends, mirror_ends, delta, delta_mirror
        )
        if core - 1 not in mates:
            blocks[core - 1] = block_bf
        solved_above = core - 1
    else:
        top_pair = call(top_products, [pair], own_gram, mirror_gram, product[-1], cost=8)
        block, block_bf, deltas = call(
            top, [vec, vec_bf, ((2, cols, width), BF)], out, received, top_pair, solved[-1]
        )
        blocks[levels - 2] = block
        received = mirrored[levels - 2] = send(block_bf, levels - 2)
        blocks[-1], mirrored[-1] = call(top_values, [vec, vec_bf], deltas, own_gram, mirror_gram)
        solved_above = levels - 2
    late = [0]
    def pass_on(level, home):
        received = send(block_bf, level, level < core)
        if home == (level < core):
            mirrored[level] = mate(received)
            late.append(level)
        else:
            mirrored[level] = received
        return received

    if joined:
        received = pass_on(solved_above, solved_above not in mates)
    for level in reversed(range(solved_above)):
        home = level not in mates
        outs = [vec, vec_bf] if home else [vec_bf]
        if level + 1 >= core:
            side = 0 if home else 1
            part = call(back_part, [vec], solved[level], block_bf, product[level], side=side)
            made = call(back, outs, part, received, product[level], side=1 - side)
        else:
            known = mate(block_bf)
            if home:
                blocks[level + 1] = known
            made = call(back_both, outs, received, known, solved[level], product[level])
        if home:
            blocks[level], block_bf = made
        else:
            block_bf = made
        received = pass_on(level, home)
    if 0 in mates:
        blocks[0] = mate(block_bf)
    early = tuple(level for level in range(levels) if level not in late)
    part = call(
        leaf_part, [((cols, size), F32)],
        leaf, leaf_inv, leaf_prod, *[mirrored[level] for level in early], early=early,
    )
    leaf_solution, stacked = call(
        finish, [((cols, size), F32), ((levels, cols, width), F32)],
        part, leaf_prod, *[mirrored[level] for level in late], *blocks, late=tuple(late),
    )
    return leaf_solution.T, jnp.swapaxes(stacked, 1, 2)[None]


def solution(mesh):
    both = ("gx", "gy")
    return jax.shard_map(
        shards,
        mesh=mesh,
        in_specs=tuple(P(both, *[None] * rank) for rank in (1, 2, 3, 3, 3, 5)),
        out_specs=(P(both, None), P(both, None, None, None)),
        check_vma=False,
    )
```

```python
import functools

import jax
import jax.numpy as jnp
from jax import lax
from jax.experimental import pallas as pl
from jax.experimental.pallas import tpu as pltpu
from jax.sharding import PartitionSpec as P

BF = jnp.bfloat16
F32 = jnp.float32
VMEM = pl.BlockSpec(memory_space=pltpu.VMEM)


def times(values, matrix):
    return lax.dot_general(values, matrix, (((1,), (0,)), ((), ())), preferred_element_type=F32)


def times_t(values, matrix):
    return lax.dot_general(values, matrix, (((1,), (1,)), ((), ())), preferred_element_type=F32)


def gram(left, right):
    return lax.dot_general(left, right, (((0,), (0,)), ((), ())), preferred_element_type=F32)


def turned(inverse, coupling):
    return lax.dot_general(inverse, coupling, (((0,), (1,)), ((), ())), preferred_element_type=F32)


def exchange(value, level, gy_levels, cross=False):
    inner, outer = lax.axis_size("gy"), lax.axis_size("gx")
    mask = 2**level ^ (inner if cross else 0)
    pairs = [(source, source ^ mask) for source in range(inner * outer)]
    return lax.ppermute(value, ("gx", "gy"), pairs)


def call(body, outs, *args, cost=1, **static):
    moved = sum(a.size * a.dtype.itemsize for a in args)
    made = pl.pallas_call(
        functools.partial(body, **static),
        out_shape=[jax.ShapeDtypeStruct(shape, kind) for shape, kind in outs],
        in_specs=[VMEM] * len(args),
        out_specs=[VMEM] * len(outs),
        compiler_params=pltpu.CompilerParams(vmem_limit_bytes=32 * 2**20),
        cost_estimate=pl.CostEstimate(flops=cost * 3 * 10**8, bytes_accessed=moved, transcendentals=0),
    )(*args)
    return made if len(outs) > 1 else made[0]


def products(inverse, coupling, out, *, level):
    for side in range(2):
        out[side] = times(coupling[level, side], inverse[level]).astype(BF)


def products_ahead(inverse, coupling, terms, ahead, *, level):
    rows = inverse.shape[1]
    ahead[:rows] = turned(inverse[level], coupling[level, 1]).astype(BF)
    ahead[rows:] = terms[level + 1].astype(BF)


def products_last(inverse, coupling, terms, values, out, out_turned, below, below_turned, folded, fixed, *, level):
    for side in range(2):
        out[side] = times(coupling[level, side], inverse[level]).astype(BF)
        below[side] = times(coupling[level - 1, side], inverse[level - 1]).astype(BF)
        out_turned[side] = turned(inverse[level], coupling[level, side]).astype(BF)
    below_turned[...] = turned(inverse[level - 1], coupling[level - 1, 0]).astype(BF)
    for side in range(2):
        folded[side] = times(below_turned[...], out_turned[side]).astype(BF)
    right = values[level].astype(BF)
    fixed[0] = values[level + 1] - times(right, out_turned[0])
    fixed[1] = terms[level + 1] + times(right, out_turned[1])


def top_gram(inverse, out):
    matrix = inverse[inverse.shape[0] - 1]
    out[...] = gram(matrix, matrix).astype(BF)


def top_products(own, mirror, product, out):
    out[0] = times(own[...], product[0]).astype(BF)
    out[1] = times(mirror[...], product[1]).astype(BF)


def forward(residue, received, product, terms, delta, out, *, level):
    change = (residue[0] - received[...].astype(F32)).astype(BF)
    delta[...] = change
    out[...] = (terms[level + 1] + times_t(change, product[1])).astype(BF)


def forward_ahead(residue, received, product, terms, values, delta, out, ahead, *, level):
    change = (residue[0] - received[...].astype(F32)).astype(BF)
    delta[...] = change
    out[...] = (terms[level + 1] + times_t(change, product[1])).astype(BF)
    ahead[...] = (values[level + 1] - times_t(change, product[0])).astype(BF)


def forward_mate(received, residue, ahead, delta, out):
    rows = ahead.shape[1]
    change = (residue[...].astype(F32) - received[...].astype(F32)).astype(BF)
    delta[...] = change
    out[...] = (ahead[rows:].astype(F32) + times(change, ahead[:rows])).astype(BF)


def forward_back(received, below, product_below, product, terms, values, delta, out, *ahead, level):
    residue = values[level] - times_t(below[...], product_below[0])
    change = (residue - received[...].astype(F32)).astype(BF)
    delta[...] = change
    out[...] = (terms[level + 1] + times_t(change, product[1])).astype(BF)
    for above in ahead:
        above[...] = (values[level + 1] - times_t(change, product[0])).astype(BF)


def forward_residue(delta, product, values, residue, *, level):
    residue[0] = values[level + 1] - times_t(delta[...], product[0])


def forward_top(residue, received, product, terms, values, delta, out, *, level):
    change = (residue[0] - received[...].astype(F32)).astype(BF)
    delta[...] = change
    rows = change.shape[0]
    out[:rows] = (terms[level + 1] + times_t(change, product[1])).astype(BF)
    out[rows:] = (values[level + 1] - times_t(change, product[0])).astype(BF)


def forward_lowest(residue, received, product, terms, values, delta, out, ahead):
    change = (residue[0] - received[...].astype(F32)).astype(BF)
    delta[...] = change
    out[...] = (terms[1] + times(change, product[1])).astype(BF)
    ahead[...] = (values[1] - times(change, product[0])).astype(BF)


def forward_last(received, below, folded, product, fixed, out):
    rows, arrived = received.shape[0], received[...].astype(BF)
    out[:rows] = (fixed[1] - times(below[...], folded[1]) - times(arrived, product[1])).astype(BF)
    out[rows:] = (fixed[0] + times(below[...], folded[0]) + times(arrived, product[0])).astype(BF)


def solve_last(received, below, below_turned, inverse, values, solved, *, level):
    residue = values[level] - times(below[...], below_turned[...])
    change = (residue - received[...].astype(F32)).astype(BF)
    step = times_t(change, inverse[level]).astype(BF)
    solved[...] = times(step, inverse[level])


def early_products(inverse, coupling, terms, pack, ahead, lowest, lowest_turned, *, level):
    width = inverse.shape[1]
    for side in range(2):
        made = times(coupling[level, side], inverse[level]).astype(BF)
        pack[side * width : (side + 1) * width] = made
        lowest[side] = times(coupling[0, side], inverse[0]).astype(BF)
        lowest_turned[side] = turned(inverse[0], coupling[0, side]).astype(BF)
    products_ahead(inverse, coupling, terms, ahead, level=1)


def top_ends(own_gram, terms, values, out):
    width, cols = own_gram.shape[0], values.shape[1]
    out[:width] = own_gram[...]
    out[width : width + cols] = values[values.shape[0] - 1].astype(BF)
    out[width + cols :] = terms[terms.shape[0] - 1].astype(BF)


def join_top(mine, mirror, ends, mirror_ends, inverse, sent, out, *, level):
    width = inverse.shape[1]
    gram_mine, gram_mirror = ends[:width], mirror_ends[:width]
    own, other = mine[:width], mine[width:]
    mirror_own, mirror_other = mirror[:width], mirror[width:]
    first = times(gram_mine, own).astype(BF)
    second = times(gram_mirror, other).astype(BF)
    matrix = inverse[level]
    out[:width] = (gram(matrix, matrix) + gram(own, first) + gram(other, second)).astype(BF)
    out[width : 2 * width] = (gram(mirror_other, first) + gram(mirror_own, second)).astype(BF)
    right, mirror_right = top_rights(ends, mirror_ends)
    cols = right.shape[0]
    out[2 * width : 2 * width + cols] = (-times(right, first) - times(mirror_right, second)).astype(BF)
    out[2 * width + cols :] = sent[...]


def top_rights(mine, mirror):
    width = mine.shape[1]
    cols = (mine.shape[0] - width) // 2
    right = mine[width : width + cols].astype(F32) - mirror[width + cols :].astype(F32)
    mirror_right = mirror[width : width + cols].astype(F32) - mine[width + cols :].astype(F32)
    return right.astype(BF), mirror_right.astype(BF)


def join_own(joined, joined_mate, solved, product, across, part, delta, folded, base, *, home):
    rows, width = part.shape[1], joined.shape[1]
    mine, mate = joined[2 * width + rows :], joined_mate[2 * width + rows :]
    for at, (a, b, matrices) in enumerate(((mine, mate, joined), (mate, mine, joined_mate))):
        change = (a[rows:].astype(F32) - b[:rows].astype(F32)).astype(BF)
        delta[at] = change
        part[at] = times(change, matrices[:width]) + matrices[2 * width : 2 * width + rows].astype(F32)
    total = solved[...]
    for side, at in enumerate((0, 1) if home else (1, 0)):
        matrices = (joined, joined_mate)[at]
        total = total - times(part[at].astype(BF), product[side])
        folded[side] = times(matrices[width : 2 * width], product[side]).astype(BF)
    first, second = (0, 1) if home else (1, 0)
    base[...] = total + times(across[:rows], folded[first]) - times(across[rows:], folded[second])


def join(theirs, base, folded, below, *, home):
    rows = base.shape[0]
    first, second = (0, 1) if home else (1, 0)
    total = base[...] - times(theirs[rows:], folded[first]) + times(theirs[:rows], folded[second])
    below[...] = total.astype(BF)


def join_blocks(theirs, across, part, joined, joined_mate, delta, block, block_mate):
    rows, width = block.shape
    for at, (a, b) in enumerate(((theirs, across), (across, theirs))):
        delta[at] = (a[rows:].astype(F32) - b[:rows].astype(F32)).astype(BF)
    block[...] = part[0] + times(delta[0], joined[width : 2 * width])
    value = part[1] + times(delta[1], joined_mate[width : 2 * width])
    block_mate[...] = value.astype(BF)


def top_blocks(mine, mirror, ends, mirror_ends, delta, delta_mirror, out, mirrored):
    width = out.shape[1]
    right, mirror_right = top_rights(ends, mirror_ends)
    change, other = delta[0], delta_mirror[0]
    own = right.astype(F32) - times_t(change, mine[:width])
    own = own - times_t(other, mirror[width:])
    theirs = mirror_right.astype(F32) - times_t(other, mirror[:width])
    theirs = theirs - times_t(change, mine[width:])
    out[...] = times(own.astype(BF), ends[:width])
    mirrored[...] = times(theirs.astype(BF), mirror_ends[:width]).astype(BF)


def solve(delta, inverse, solved, *, level):
    step = times_t(delta[...], inverse[level]).astype(BF)
    solved[...] = times(step, inverse[level])


def top(mine, received, product, solved, out, out_bf, delta):
    rows = solved.shape[0]
    own = (mine[rows:].astype(F32) - received[:rows].astype(F32)).astype(BF)
    other = (received[rows:].astype(F32) - mine[:rows].astype(F32)).astype(BF)
    value = solved[...] - times(own, product[0]) - times(other, product[1])
    out[...] = value
    out_bf[...] = value.astype(BF)
    delta[0] = own
    delta[1] = other


def top_values(delta, own, mirror, out, mirrored):
    out[...] = times(delta[0], own[...])
    mirrored[...] = times(delta[1], mirror[...]).astype(BF)


def back_part(solved, known, product, out, *, side):
    out[...] = solved[...] - times(known[...].astype(BF), product[side])


def back(part, received, product, *outs, side):
    value = part[...] - times(received[...].astype(BF), product[side])
    for out in outs:
        out[...] = value.astype(out.dtype)


def back_both(received, known, solved, product, *outs):
    value = solved[...] - times(known[...], product[0])
    value = value - times(received[...].astype(BF), product[1])
    for out in outs:
        out[...] = value.astype(out.dtype)


def leaf_part(leaf, inverse, leaf_products, *refs, early):
    *mirrored, out = refs
    total = times(leaf[...].astype(BF), inverse[...])
    for level, block in zip(early, mirrored, strict=True):
        total = total - times(block[...], leaf_products[level])
    out[...] = total


def finish(part, leaf_products, *refs, late):
    *refs, leaf, out = refs
    mirrored, blocks = refs[: len(late)], refs[len(late) :]
    total = part[...]
    for level, block in zip(late, mirrored, strict=True):
        total = total - times(block[...].astype(BF), leaf_products[level])
    leaf[...] = total
    for level, block in enumerate(blocks):
        out[level] = block[...].astype(F32)


def shards(leaf_values, leaf_inverse, leaf_coupling, block_values, block_inverse, block_coupling):
    levels, width = block_inverse.shape[1], block_inverse.shape[2]
    size, cols = leaf_values.shape
    core = lax.axis_size("gy").bit_length() - 1
    inverse, coupling = block_inverse[0], block_coupling[0, :, 0]
    leaf_inv, leaf_cpl = leaf_inverse[0], leaf_coupling[0]
    values = jnp.swapaxes(block_values[0], 1, 2)
    vec, vec_bf, pair = ((cols, width), F32), ((cols, width), BF), ((2, width, width), BF)
    slab = ((1, cols, width), F32)

    def send(value, level, cross=False):
        return exchange(value, level, core, cross)

    def mate(value):
        return exchange(value, core, core)

    def arrived(value):
        return value.astype(F32)

    def after(value, other):
        return lax.optimization_barrier((value, other))[0]

    below_top = levels - 1
    first_across = 1 + (core - 1) % 2
    at_home = [
        level < first_across or level >= core or (level - first_across) % 2 == 1
        for level in range(levels)
    ]
    leaf = times_t(leaf_values.T.astype(BF), leaf_inv)
    terms = jnp.einsum("kwn,rn->krw", leaf_cpl, leaf.astype(BF), preferred_element_type=F32)
    received = send(terms[0].astype(BF), 0)
    product, ahead, solved = [None] * below_top, [None] * below_top, [None] * below_top
    joined = levels == core + 2 and core >= 3 and core % 2 == 1
    own_gram = call(top_gram, [((width, width), BF)], inverse)
    inverse_later = after(inverse, own_gram)
    if joined:
        pack, ahead[1], product[0], lowest = call(
            early_products, [((2 * width, width), BF), ((width + cols, width), BF), pair, pair],
            inverse_later, coupling, terms, level=core,
        )
        mirror_pack = send(pack, below_top)
        inverse_later = after(inverse, pack)
        ends = call(top_ends, [((width + 2 * cols, width), BF)], own_gram, terms, values, cost=0)
    for level in range(1 if joined else 0, core - 2 if joined else below_top):
        product[level] = call(
            products, [pair], inverse_later, coupling, level=level
        )
    for level in range(core):
        if not at_home[level] and ahead[level] is None:
            ahead[level] = call(
                products_ahead, [((width + cols, width), BF)], inverse_later, coupling, terms, level=level
            )

    residue, change = values, None
    for level in range(core if joined else below_top):
        below = change
        if joined and level == core - 1:
            below, mirror_pack = lax.optimization_barrier((below, mirror_pack))
            last = arrived(received)
            out = call(
                forward_last, [((2 * cols, width), BF)],
                last, below, folded, last_turned, fixed, cost=4,
            )
            received = send(out, below_top, True)
        elif level == levels - 2:
            received, mirror_gram = lax.optimization_barrier((received, mirror_gram))
            change, out = call(
                forward_top, [vec_bf, ((2 * cols, width), BF)],
                residue, received, product[level], terms, values, level=level,
            )
            received = send(out, below_top)
        else:
            across = first_across <= level + 1 < core
            if not at_home[level]:
                if joined and level == core - 2:
                    ahead[level], ends = lax.optimization_barrier((ahead[level], ends))
                change, out = call(
                    forward_mate, [vec_bf, vec_bf], received, residue, ahead[level], cost=2
                )
            elif level and not at_home[level - 1]:
                change, out, *above = call(
                    forward_back, [vec_bf, vec_bf] + ([] if at_home[level + 1] else [vec_bf]),
                    arrived(received), below, product[level - 1], product[level], terms, values, level=level,
                )
                residue = above[0] if above else None
            elif joined and level == 0:
                change, out, residue = call(
                    forward_lowest, [vec_bf, vec_bf, vec_bf],
                    residue, received, lowest, terms, values, cost=0,
                )
            elif not at_home[level + 1]:
                change, out, residue = call(
                    forward_ahead, [vec_bf, vec_bf, vec_bf],
                    residue, received, product[level], terms, values, level=level,
                )
            else:
                change, out = call(
                    forward, [vec_bf, vec_bf], residue, received, product[level], terms, level=level
                )
            received = send(out, level + 1, across)
            if joined and level == core - 2:
                product[core - 1], last_turned, product[core - 2], below_turned, folded, fixed = call(
                    products_last,
                    [pair, pair, pair, ((width, width), BF), pair, ((2, cols, width), F32)],
                    after(inverse, out), coupling, terms, values, level=core - 1, cost=1,
                )
            if level == 0:
                if joined:
                    mirror_ends = send(after(ends, out), below_top)
                else:
                    mirror_gram = send(after(own_gram, out), below_top)
            if not at_home[level]:
                change = mate(change)
            elif not at_home[level + 1]:
                residue = mate(residue)
                ahead[level + 1] = mate(after(ahead[level + 1], out))
            else:
                residue = call(
                    forward_residue, [slab], change, product[level], values, level=level, cost=0
                )
        if joined and level == core - 1:
            solved[level] = call(
                solve_last, [vec], last, below, below_turned, inverse, values, level=level, cost=12
            )
        else:
            solved[level] = call(solve, [vec], change, inverse, level=level)
    leaf_prod = jnp.einsum("kwn,nm->kwm", leaf_cpl, leaf_inv, preferred_element_type=F32).astype(BF)

    mates = [level for level in range(core) if level % 2 == 0]
    for level in mates:
        product[level] = mate(after(product[level], out))
        solved[level] = mate(after(solved[level], out))
    blocks, mirrored = [None] * levels, [None] * levels
    if joined:
        mirror_ends = after(mirror_ends, out)
        matrices = call(
            join_top, [((2 * width + 3 * cols, width), BF)],
            pack, mirror_pack, ends, mirror_ends, inverse, out, level=core, cost=1,
        )
        matrices_mate = mate(matrices)
        both, both_bf = ((2, cols, width), F32), ((2, cols, width), BF)
        at_own = core - 1 not in mates
        part, delta, folded, base = call(
            join_own, [both, both_bf, pair, vec],
            matrices, matrices_mate, solved[core - 1], product[core - 1], received, home=at_own, cost=9,
        )
        theirs = mate(received)
        block_bf = call(join, [vec_bf], theirs, base, folded, home=at_own)
        delta_mirror, blocks[core], mirrored[core] = call(
            join_blocks, [both_bf, vec, vec_bf], theirs, received, part, matrices, matrices_mate
        )
        blocks[-1], mirrored[-1] = call(
            top_blocks, [vec, vec_bf], pack, mirror_pack, ends, mirror_ends, delta, delta_mirror
        )
        if core - 1 not in mates:
            blocks[core - 1] = block_bf
        solved_above = core - 1
    else:
        top_pair = call(top_products, [pair], own_gram, mirror_gram, product[-1], cost=8)
        block, block_bf, deltas = call(
            top, [vec, vec_bf, ((2, cols, width), BF)], out, received, top_pair, solved[-1]
        )
        blocks[levels - 2] = block
        received = mirrored[levels - 2] = send(block_bf, levels - 2)
        blocks[-1], mirrored[-1] = call(top_values, [vec, vec_bf], deltas, own_gram, mirror_gram)
        solved_above = levels - 2
    late = [0]
    def pass_on(level, home):
        received = send(block_bf, level, level < core)
        if home == (level < core):
            mirrored[level] = mate(received)
            late.append(level)
        else:
            mirrored[level] = received
        return received

    if joined:
        received = pass_on(solved_above, solved_above not in mates)
    for level in reversed(range(solved_above)):
        home = level not in mates
        outs = [vec, vec_bf] if home else [vec_bf]
        if level + 1 >= core:
            side = 0 if home else 1
            part = call(back_part, [vec], solved[level], block_bf, product[level], side=side)
            made = call(back, outs, part, received, product[level], side=1 - side)
        else:
            known = mate(block_bf)
            if home:
                blocks[level + 1] = known
            made = call(back_both, outs, received, known, solved[level], product[level])
        if home:
            blocks[level], block_bf = made
        else:
            block_bf = made
        received = pass_on(level, home)
    if 0 in mates:
        blocks[0] = mate(block_bf)
    early = tuple(level for level in range(levels) if level not in late)
    part = call(
        leaf_part, [((cols, size), F32)],
        leaf, leaf_inv, leaf_prod, *[mirrored[level] for level in early], early=early,
    )
    leaf_solution, stacked = call(
        finish, [((cols, size), F32), ((levels, cols, width), F32)],
        part, leaf_prod, *[mirrored[level] for level in late], *blocks, late=tuple(late),
    )
    return leaf_solution.T, jnp.swapaxes(stacked, 1, 2)[None]


def solution(mesh):
    both = ("gx", "gy")
    return jax.shard_map(
        shards,
        mesh=mesh,
        in_specs=tuple(P(both, *[None] * rank) for rank in (1, 2, 3, 3, 3, 5)),
        out_specs=(P(both, None), P(both, None, None, None)),
        check_vma=False,
    )
```

```python
import functools

import jax
import jax.numpy as jnp
from jax import lax
from jax.experimental import pallas as pl
from jax.experimental.pallas import tpu as pltpu
from jax.sharding import PartitionSpec as P

BF = jnp.bfloat16
F32 = jnp.float32
VMEM = pl.BlockSpec(memory_space=pltpu.VMEM)


def times(values, matrix):
    return lax.dot_general(values, matrix, (((1,), (0,)), ((), ())), preferred_element_type=F32)


def times_t(values, matrix):
    return lax.dot_general(values, matrix, (((1,), (1,)), ((), ())), preferred_element_type=F32)


def gram(left, right):
    return lax.dot_general(left, right, (((0,), (0,)), ((), ())), preferred_element_type=F32)


def deep(first, second, matrices):
    depth, width = matrices.shape[1:]
    return times(jnp.concatenate([first, second], axis=1), matrices[...].reshape(2 * depth, width))


def turned(inverse, coupling):
    return lax.dot_general(inverse, coupling, (((0,), (1,)), ((), ())), preferred_element_type=F32)


def exchange(value, level, gy_levels, cross=False):
    inner, outer = lax.axis_size("gy"), lax.axis_size("gx")
    mask = 2**level ^ (inner if cross else 0)
    pairs = [(source, source ^ mask) for source in range(inner * outer)]
    return lax.ppermute(value, ("gx", "gy"), pairs)


def call(body, outs, *args, cost=1, **static):
    moved = sum(a.size * a.dtype.itemsize for a in args)
    made = pl.pallas_call(
        functools.partial(body, **static),
        out_shape=[jax.ShapeDtypeStruct(shape, kind) for shape, kind in outs],
        in_specs=[VMEM] * len(args),
        out_specs=[VMEM] * len(outs),
        compiler_params=pltpu.CompilerParams(vmem_limit_bytes=32 * 2**20),
        cost_estimate=pl.CostEstimate(flops=cost * 3 * 10**8, bytes_accessed=moved, transcendentals=0),
    )(*args)
    return made if len(outs) > 1 else made[0]


def products(inverse, coupling, out, *, level):
    for side in range(2):
        out[side] = times(coupling[level, side], inverse[level]).astype(BF)


def products_ahead(inverse, coupling, terms, ahead, *, level):
    rows = inverse.shape[1]
    ahead[:rows] = turned(inverse[level], coupling[level, 1]).astype(BF)
    ahead[rows:] = terms[level + 1].astype(BF)


def products_last(inverse, coupling, terms, values, out, below, below_turned, maps, fixed, *, level):
    for side in range(2):
        out[side] = times(coupling[level, side], inverse[level]).astype(BF)
        below[side] = times(coupling[level - 1, side], inverse[level - 1]).astype(BF)
        maps[side, 1] = turned(inverse[level], coupling[level, side]).astype(BF)
    below_turned[...] = turned(inverse[level - 1], coupling[level - 1, 0]).astype(BF)
    for side in range(2):
        maps[side, 0] = times(below_turned[...], maps[side, 1]).astype(BF)
    right = values[level].astype(BF)
    fixed[0] = values[level + 1] - times(right, maps[0, 1])
    fixed[1] = terms[level + 1] + times(right, maps[1, 1])


def top_gram(inverse, out):
    matrix = inverse[inverse.shape[0] - 1]
    out[...] = gram(matrix, matrix).astype(BF)


def top_products(own, mirror, product, out):
    out[0] = times(own[...], product[0]).astype(BF)
    out[1] = times(mirror[...], product[1]).astype(BF)


def forward(residue, received, product, terms, delta, out, *, level):
    change = (residue[0] - received[...].astype(F32)).astype(BF)
    delta[...] = change
    out[...] = (terms[level + 1] + times_t(change, product[1])).astype(BF)


def forward_ahead(residue, received, product, terms, values, delta, out, ahead, *, level):
    change = (residue[0] - received[...].astype(F32)).astype(BF)
    delta[...] = change
    out[...] = (terms[level + 1] + times_t(change, product[1])).astype(BF)
    ahead[...] = (values[level + 1] - times_t(change, product[0])).astype(BF)


def forward_mate(received, residue, ahead, delta, out):
    rows = ahead.shape[1]
    change = (residue[...].astype(F32) - received[...].astype(F32)).astype(BF)
    delta[...] = change
    out[...] = (ahead[rows:].astype(F32) + times(change, ahead[:rows])).astype(BF)


def forward_back(received, below, product_below, product, terms, values, delta, out, *ahead, level):
    residue = values[level] - times_t(below[...], product_below[0])
    change = (residue - received[...].astype(F32)).astype(BF)
    delta[...] = change
    out[...] = (terms[level + 1] + times_t(change, product[1])).astype(BF)
    for above in ahead:
        above[...] = (values[level + 1] - times_t(change, product[0])).astype(BF)


def forward_residue(delta, product, values, residue, *, level):
    residue[0] = values[level + 1] - times_t(delta[...], product[0])


def forward_top(residue, received, product, terms, values, delta, out, *, level):
    change = (residue[0] - received[...].astype(F32)).astype(BF)
    delta[...] = change
    rows = change.shape[0]
    out[:rows] = (terms[level + 1] + times_t(change, product[1])).astype(BF)
    out[rows:] = (values[level + 1] - times_t(change, product[0])).astype(BF)


def forward_lowest(residue, received, product, terms, values, delta, out, ahead):
    change = (residue[0] - received[...].astype(F32)).astype(BF)
    delta[...] = change
    out[...] = (terms[1] + times(change, product[1])).astype(BF)
    ahead[...] = (values[1] - times(change, product[0])).astype(BF)


def forward_last(received, below, maps, fixed, out):
    rows, arrived = received.shape[0], received[...].astype(BF)
    out[:rows] = (fixed[1] - deep(below[...], arrived, maps[1])).astype(BF)
    out[rows:] = (fixed[0] + deep(below[...], arrived, maps[0])).astype(BF)


def solve_last(received, below, below_turned, inverse, values, solved, *, level):
    residue = values[level] - times(below[...], below_turned[...])
    change = (residue - received[...].astype(F32)).astype(BF)
    step = times_t(change, inverse[level]).astype(BF)
    solved[...] = times(step, inverse[level])


def early_products(inverse, coupling, terms, pack, ahead, lowest, lowest_turned, *, level):
    width = inverse.shape[1]
    for side in range(2):
        made = times(coupling[level, side], inverse[level]).astype(BF)
        pack[side * width : (side + 1) * width] = made
        lowest[side] = times(coupling[0, side], inverse[0]).astype(BF)
        lowest_turned[side] = turned(inverse[0], coupling[0, side]).astype(BF)
    products_ahead(inverse, coupling, terms, ahead, level=1)


def top_ends(own_gram, terms, values, out):
    width, cols = own_gram.shape[0], values.shape[1]
    out[:width] = own_gram[...]
    out[width : width + cols] = values[values.shape[0] - 1].astype(BF)
    out[width + cols :] = terms[terms.shape[0] - 1].astype(BF)


def join_top(mine, mirror, ends, mirror_ends, inverse, sent, out, *, level):
    width = inverse.shape[1]
    gram_mine, gram_mirror = ends[:width], mirror_ends[:width]
    own, other = mine[:width], mine[width:]
    mirror_own, mirror_other = mirror[:width], mirror[width:]
    first = times(gram_mine, own).astype(BF)
    second = times(gram_mirror, other).astype(BF)
    matrix = inverse[level]
    out[:width] = (gram(matrix, matrix) + gram(own, first) + gram(other, second)).astype(BF)
    out[width : 2 * width] = (gram(mirror_other, first) + gram(mirror_own, second)).astype(BF)
    right, mirror_right = top_rights(ends, mirror_ends)
    cols = right.shape[0]
    out[2 * width : 2 * width + cols] = (-times(right, first) - times(mirror_right, second)).astype(BF)
    out[2 * width + cols :] = sent[...]


def top_rights(mine, mirror):
    width = mine.shape[1]
    cols = (mine.shape[0] - width) // 2
    right = mine[width : width + cols].astype(F32) - mirror[width + cols :].astype(F32)
    mirror_right = mirror[width : width + cols].astype(F32) - mine[width + cols :].astype(F32)
    return right.astype(BF), mirror_right.astype(BF)


def join_own(joined, joined_mate, solved, product, across, part, delta, folded, base, *, home):
    rows, width = part.shape[1], joined.shape[1]
    mine, mate = joined[2 * width + rows :], joined_mate[2 * width + rows :]
    for at, (a, b, matrices) in enumerate(((mine, mate, joined), (mate, mine, joined_mate))):
        change = (a[rows:].astype(F32) - b[:rows].astype(F32)).astype(BF)
        delta[at] = change
        part[at] = times(change, matrices[:width]) + matrices[2 * width : 2 * width + rows].astype(F32)
    total = solved[...]
    for side, at in enumerate((0, 1) if home else (1, 0)):
        matrices = (joined, joined_mate)[at]
        total = total - times(part[at].astype(BF), product[side])
        folded[side] = times(matrices[width : 2 * width], product[side]).astype(BF)
    first, second = (0, 1) if home else (1, 0)
    base[...] = total + times(across[:rows], folded[first]) - times(across[rows:], folded[second])


def join(theirs, base, folded, below, *, home):
    rows = base.shape[0]
    first, second = (0, 1) if home else (1, 0)
    total = base[...] - times(theirs[rows:], folded[first]) + times(theirs[:rows], folded[second])
    below[...] = total.astype(BF)


def join_blocks(theirs, across, part, joined, joined_mate, delta, block, block_mate):
    rows, width = block.shape
    for at, (a, b) in enumerate(((theirs, across), (across, theirs))):
        delta[at] = (a[rows:].astype(F32) - b[:rows].astype(F32)).astype(BF)
    block[...] = part[0] + times(delta[0], joined[width : 2 * width])
    value = part[1] + times(delta[1], joined_mate[width : 2 * width])
    block_mate[...] = value.astype(BF)


def top_blocks(mine, mirror, ends, mirror_ends, delta, delta_mirror, out, mirrored):
    width = out.shape[1]
    right, mirror_right = top_rights(ends, mirror_ends)
    change, other = delta[0], delta_mirror[0]
    own = right.astype(F32) - times_t(change, mine[:width])
    own = own - times_t(other, mirror[width:])
    theirs = mirror_right.astype(F32) - times_t(other, mirror[:width])
    theirs = theirs - times_t(change, mine[width:])
    out[...] = times(own.astype(BF), ends[:width])
    mirrored[...] = times(theirs.astype(BF), mirror_ends[:width]).astype(BF)


def solve(delta, inverse, solved, *, level):
    step = times_t(delta[...], inverse[level]).astype(BF)
    solved[...] = times(step, inverse[level])


def top(mine, received, product, solved, out, out_bf, delta):
    rows = solved.shape[0]
    own = (mine[rows:].astype(F32) - received[:rows].astype(F32)).astype(BF)
    other = (received[rows:].astype(F32) - mine[:rows].astype(F32)).astype(BF)
    value = solved[...] - times(own, product[0]) - times(other, product[1])
    out[...] = value
    out_bf[...] = value.astype(BF)
    delta[0] = own
    delta[1] = other


def top_values(delta, own, mirror, out, mirrored):
    out[...] = times(delta[0], own[...])
    mirrored[...] = times(delta[1], mirror[...]).astype(BF)


def back_part(solved, known, product, out, *, side):
    out[...] = solved[...] - times(known[...].astype(BF), product[side])


def back(part, received, product, *outs, side):
    value = part[...] - times(received[...].astype(BF), product[side])
    for out in outs:
        out[...] = value.astype(out.dtype)


def back_both(received, known, solved, product, *outs):
    value = solved[...] - deep(known[...], received[...].astype(BF), product)
    for out in outs:
        out[...] = value.astype(out.dtype)


def leaf_part(leaf, inverse, leaf_products, *refs, early):
    *mirrored, out = refs
    total = times(leaf[...].astype(BF), inverse[...])
    for level, block in zip(early, mirrored, strict=True):
        total = total - times(block[...], leaf_products[level])
    out[...] = total


def finish(part, leaf_products, *refs, late):
    *refs, leaf, out = refs
    mirrored, blocks = refs[: len(late)], refs[len(late) :]
    total = part[...]
    for level, block in zip(late, mirrored, strict=True):
        total = total - times(block[...].astype(BF), leaf_products[level])
    leaf[...] = total
    for level, block in enumerate(blocks):
        out[level] = block[...].astype(F32)


def shards(leaf_values, leaf_inverse, leaf_coupling, block_values, block_inverse, block_coupling):
    levels, width = block_inverse.shape[1], block_inverse.shape[2]
    size, cols = leaf_values.shape
    core = lax.axis_size("gy").bit_length() - 1
    inverse, coupling = block_inverse[0], block_coupling[0, :, 0]
    leaf_inv, leaf_cpl = leaf_inverse[0], leaf_coupling[0]
    values = jnp.swapaxes(block_values[0], 1, 2)
    vec, vec_bf, pair = ((cols, width), F32), ((cols, width), BF), ((2, width, width), BF)
    slab = ((1, cols, width), F32)

    def send(value, level, cross=False):
        return exchange(value, level, core, cross)

    def mate(value):
        return exchange(value, core, core)

    def arrived(value):
        return value.astype(F32)

    def after(value, other):
        return lax.optimization_barrier((value, other))[0]

    below_top = levels - 1
    first_across = 1 + (core - 1) % 2
    at_home = [
        level < first_across or level >= core or (level - first_across) % 2 == 1
        for level in range(levels)
    ]
    leaf = times_t(leaf_values.T.astype(BF), leaf_inv)
    terms = jnp.einsum("kwn,rn->krw", leaf_cpl, leaf.astype(BF), preferred_element_type=F32)
    received = send(terms[0].astype(BF), 0)
    product, ahead, solved = [None] * below_top, [None] * below_top, [None] * below_top
    joined = levels == core + 2 and core >= 3 and core % 2 == 1
    own_gram = call(top_gram, [((width, width), BF)], inverse)
    inverse_later = after(inverse, own_gram)
    if joined:
        pack, ahead[1], product[0], lowest = call(
            early_products, [((2 * width, width), BF), ((width + cols, width), BF), pair, pair],
            inverse_later, coupling, terms, level=core,
        )
        mirror_pack = send(pack, below_top)
        inverse_later = after(inverse, pack)
        ends = call(top_ends, [((width + 2 * cols, width), BF)], own_gram, terms, values, cost=0)
    for level in range(1 if joined else 0, core - 2 if joined else below_top):
        product[level] = call(
            products, [pair], inverse_later, coupling, level=level
        )
    for level in range(core):
        if not at_home[level] and ahead[level] is None:
            ahead[level] = call(
                products_ahead, [((width + cols, width), BF)], inverse_later, coupling, terms, level=level
            )

    residue, change = values, None
    for level in range(core if joined else below_top):
        below = change
        if joined and level == core - 1:
            below, mirror_pack = lax.optimization_barrier((below, mirror_pack))
            last = arrived(received)
            out = call(
                forward_last, [((2 * cols, width), BF)],
                last, below, maps, fixed, cost=4,
            )
            received = send(out, below_top, True)
        elif level == levels - 2:
            received, mirror_gram = lax.optimization_barrier((received, mirror_gram))
            change, out = call(
                forward_top, [vec_bf, ((2 * cols, width), BF)],
                residue, received, product[level], terms, values, level=level,
            )
            received = send(out, below_top)
        else:
            across = first_across <= level + 1 < core
            if not at_home[level]:
                if joined and level == core - 2:
                    ahead[level], ends = lax.optimization_barrier((ahead[level], ends))
                change, out = call(
                    forward_mate, [vec_bf, vec_bf], received, residue, ahead[level], cost=2
                )
            elif level and not at_home[level - 1]:
                change, out, *above = call(
                    forward_back, [vec_bf, vec_bf] + ([] if at_home[level + 1] else [vec_bf]),
                    arrived(received), below, product[level - 1], product[level], terms, values, level=level,
                )
                residue = above[0] if above else None
            elif joined and level == 0:
                change, out, residue = call(
                    forward_lowest, [vec_bf, vec_bf, vec_bf],
                    residue, received, lowest, terms, values, cost=0,
                )
            elif not at_home[level + 1]:
                change, out, residue = call(
                    forward_ahead, [vec_bf, vec_bf, vec_bf],
                    residue, received, product[level], terms, values, level=level,
                )
            else:
                change, out = call(
                    forward, [vec_bf, vec_bf], residue, received, product[level], terms, level=level
                )
            received = send(out, level + 1, across)
            if joined and level == core - 2:
                product[core - 1], product[core - 2], below_turned, maps, fixed = call(
                    products_last,
                    [pair, pair, ((width, width), BF), ((2, 2, width, width), BF), ((2, cols, width), F32)],
                    after(inverse, out), coupling, terms, values, level=core - 1, cost=1,
                )
            if level == 0:
                if joined:
                    mirror_ends = send(after(ends, out), below_top)
                else:
                    mirror_gram = send(after(own_gram, out), below_top)
            if not at_home[level]:
                change = mate(change)
            elif not at_home[level + 1]:
                residue = mate(residue)
                ahead[level + 1] = mate(after(ahead[level + 1], out))
            else:
                residue = call(
                    forward_residue, [slab], change, product[level], values, level=level, cost=0
                )
        if joined and level == core - 1:
            solved[level] = call(
                solve_last, [vec], last, below, below_turned, inverse, values, level=level, cost=12
            )
        else:
            solved[level] = call(solve, [vec], change, inverse, level=level)
    leaf_prod = jnp.einsum("kwn,nm->kwm", leaf_cpl, leaf_inv, preferred_element_type=F32).astype(BF)

    mates = [level for level in range(core) if level % 2 == 0]
    for level in mates:
        product[level] = mate(after(product[level], out))
        solved[level] = mate(after(solved[level], out))
    blocks, mirrored = [None] * levels, [None] * levels
    if joined:
        mirror_ends = after(mirror_ends, out)
        matrices = call(
            join_top, [((2 * width + 3 * cols, width), BF)],
            pack, mirror_pack, ends, mirror_ends, inverse, out, level=core, cost=1,
        )
        matrices_mate = mate(matrices)
        both, both_bf = ((2, cols, width), F32), ((2, cols, width), BF)
        at_own = core - 1 not in mates
        part, delta, folded, base = call(
            join_own, [both, both_bf, pair, vec],
            matrices, matrices_mate, solved[core - 1], product[core - 1], received, home=at_own, cost=9,
        )
        theirs = mate(received)
        block_bf = call(join, [vec_bf], theirs, base, folded, home=at_own)
        delta_mirror, blocks[core], mirrored[core] = call(
            join_blocks, [both_bf, vec, vec_bf], theirs, received, part, matrices, matrices_mate
        )
        blocks[-1], mirrored[-1] = call(
            top_blocks, [vec, vec_bf], pack, mirror_pack, ends, mirror_ends, delta, delta_mirror
        )
        if core - 1 not in mates:
            blocks[core - 1] = block_bf
        solved_above = core - 1
    else:
        top_pair = call(top_products, [pair], own_gram, mirror_gram, product[-1], cost=8)
        block, block_bf, deltas = call(
            top, [vec, vec_bf, ((2, cols, width), BF)], out, received, top_pair, solved[-1]
        )
        blocks[levels - 2] = block
        received = mirrored[levels - 2] = send(block_bf, levels - 2)
        blocks[-1], mirrored[-1] = call(top_values, [vec, vec_bf], deltas, own_gram, mirror_gram)
        solved_above = levels - 2
    late = [0]
    def pass_on(level, home):
        received = send(block_bf, level, level < core)
        if home == (level < core):
            mirrored[level] = mate(received)
            late.append(level)
        else:
            mirrored[level] = received
        return received

    if joined:
        received = pass_on(solved_above, solved_above not in mates)
    for level in reversed(range(solved_above)):
        home = level not in mates
        outs = [vec, vec_bf] if home else [vec_bf]
        if level + 1 >= core:
            side = 0 if home else 1
            part = call(back_part, [vec], solved[level], block_bf, product[level], side=side)
            made = call(back, outs, part, received, product[level], side=1 - side)
        else:
            known = mate(block_bf)
            if home:
                blocks[level + 1] = known
            made = call(back_both, outs, received, known, solved[level], product[level])
        if home:
            blocks[level], block_bf = made
        else:
            block_bf = made
        received = pass_on(level, home)
    if 0 in mates:
        blocks[0] = mate(block_bf)
    early = tuple(level for level in range(levels) if level not in late)
    part = call(
        leaf_part, [((cols, size), F32)],
        leaf, leaf_inv, leaf_prod, *[mirrored[level] for level in early], early=early,
    )
    leaf_solution, stacked = call(
        finish, [((cols, size), F32), ((levels, cols, width), F32)],
        part, leaf_prod, *[mirrored[level] for level in late], *blocks, late=tuple(late),
    )
    return leaf_solution.T, jnp.swapaxes(stacked, 1, 2)[None]


def solution(mesh):
    both = ("gx", "gy")
    return jax.shard_map(
        shards,
        mesh=mesh,
        in_specs=tuple(P(both, *[None] * rank) for rank in (1, 2, 3, 3, 3, 5)),
        out_specs=(P(both, None), P(both, None, None, None)),
        check_vma=False,
    )
```
